32 devices in a mesh: rep: 2 (over y), dp: 4 (over z), tp: 4 (over x, core).
Axes of the slice: x: 2, y: 2, z: 4, core: 2. Of those that a mesh axis runs over, the one named last changes fastest.
Arguments:
- attention_input: bfloat16 [2048, 8192], P(('rep', 'dp'), 'tp'), parts along dimension 0, may hold values from -6 to 6
- output_weight: bfloat16 [8192, 4096], P('tp'), may hold values from -0.09375 to 0.09375
- adapter_down_weight: bfloat16 [16, 8192, 64], P('dp', 'tp'), may hold values from -0.0625 to 0.0625
- adapter_up_weight: bfloat16 [16, 64, 4096], P('dp', None, 'tp'), may hold values from -0.75 to 0.75
- fetched_local_numbers: int32 [8, 4, 2], P('rep'), parts along dimension 0, may hold values from 0 to 3, as said below
- request_adapter_entry: int32 [2048], P(('rep', 'dp')), parts along dimension 0, may hold values from 0 to 7, as said below
Outputs:
- projected: bfloat16 [2048, 4096], P(('rep', 'dp'), 'tp'), parts along dimension 0
The draws below stay inside these ranges and needn't reach their ends.
There are 2 independent parts, one for each index of `rep`. The reference program is written for one: setup_inputs(seed, part) draws one part's arguments, and reference() takes and returns one part's arrays. A program takes and returns all parts, laid end to end along the dimension named above; an argument that names none is the same for every part. Nothing has to cross between parts.
Inputs may be any that keep to these rules, and one draw needn't show every extreme that they name: `fetched_local_numbers`: for each g and o the 2 entries are different local numbers. `request_adapter_entry`: among the 256 requests of one index of dp at most 128 name one owner, and one owner is named exactly 128 times.
All inputs are finite; a program needn't handle non-finite values.
Results may differ from the reference program's by a relative error of at most 0.001.
Values may be sent and summed in bfloat16 or wider, within the bound.
A program may use at most 64 MiB of HBM per device.

```python
import jax
import jax.numpy as jnp
from jax import lax

QUERY_FEATURES = 8192
OUTPUT_FEATURES = 4096
ADAPTER_RANK = 64
ADP_DEV = 4
CAP = 2
REQ_DEV = 256
REQS = 1024
ADAPTER_TOTAL = 16
RCAP = 128
N_DP = 4


def draw_fetched_local_numbers(key, part):
    key = jax.random.fold_in(key, 11)
    scores = jax.random.randint(key, (N_DP, N_DP, ADP_DEV), 0, 1 << 20)
    scores = scores * ADP_DEV + jnp.arange(ADP_DEV, dtype=jnp.int32)
    ranking = jnp.argsort(scores, axis=-1)
    return ranking[:, :, :CAP].astype(jnp.int32)


def draw_request_adapter_entry(key, part):
    key = jax.random.fold_in(key, 23)

    def one_group(group_key):
        sub_keys = jax.random.split(group_key, 4)
        busiest = jax.random.randint(sub_keys[0], (), 0, N_DP)
        others = (busiest + 1 + jnp.arange(N_DP - 1, dtype=jnp.int32)) % N_DP
        owner_pool = jnp.repeat(others, RCAP)
        shuffled = owner_pool[jax.random.permutation(sub_keys[1], owner_pool.shape[0])]
        owners = jnp.concatenate([jnp.full((RCAP,), busiest, jnp.int32), shuffled[:REQ_DEV - RCAP]])
        owners = owners[jax.random.permutation(sub_keys[2], REQ_DEV)]
        within = jax.random.randint(sub_keys[3], (REQ_DEV,), 0, CAP)
        return owners * CAP + within
    return jax.vmap(one_group)(jax.random.split(key, N_DP)).reshape(REQ_DEV * N_DP).astype(jnp.int32)


def raised(values, stream_key, source, target, parts, factor):
    def block_of(axis_at):
        return (jnp.arange(values.shape[axis_at]) // (values.shape[axis_at] // parts)).reshape((-1,) + (1,) * (values.ndim - 1 - axis_at))

    one_side = jax.random.permutation(stream_key, parts)[block_of(target)]
    far = (block_of(target) + parts // 2) % parts
    return jnp.where((block_of(source) == one_side) | (block_of(source) == far), factor * values, values)


def block_levels(own_key, extent, shards, low, largest):
    def one(position, parts):
        steps = jax.random.uniform(jax.random.fold_in(jax.random.fold_in(own_key, 6), position), (parts,), jnp.float32, low / len(shards), largest / len(shards))
        return jnp.repeat(jnp.exp(steps), extent[position] // parts).reshape((-1,) + (1,) * (len(extent) - position - 1))

    loudness = one(*shards[0])
    for cut in shards[1:]:
        loudness = loudness * one(*cut)
    return loudness


def scatter_about(key, extent, scale, most, pieces=(), kind=jnp.bfloat16):
    level = block_levels(key, extent, pieces, -0.22, 0.18) if pieces else 1.0
    values = jax.random.normal(key, extent, jnp.float32) * scale * level
    return jnp.minimum(jnp.maximum(values, -most), most).astype(kind)


def heavy_noise(key, extent, spread, limit, cuts, heavy, kind=jnp.bfloat16):
    entries = spread * jax.random.normal(key, extent, jnp.float32)
    if cuts:
        entries = entries * block_levels(key, extent, cuts, -0.22, 0.18)
    return jnp.clip(raised(entries, jax.random.fold_in(key, 3), *heavy), -limit, limit).astype(kind)


def setup_inputs(seed: int = 0, part: int = 0) -> dict:
    keys = jax.random.split(jax.random.key(seed), 7)
    part_keys = jax.random.split(jax.random.fold_in(keys[6], part), 7)
    return {
        "attention_input": scatter_about(part_keys[0], (REQS, QUERY_FEATURES), 1.0, 6.0, ((0, 4), (1, 4))),
        "output_weight": heavy_noise(keys[1], (QUERY_FEATURES, OUTPUT_FEATURES), QUERY_FEATURES ** -0.5, 0.09375, ((0, 4),), (0, 1, 4, 2.0)),
        "adapter_down_weight": scatter_about(keys[2], (ADAPTER_TOTAL, QUERY_FEATURES, ADAPTER_RANK), QUERY_FEATURES ** -0.5, 0.0625, ((0, 4), (1, 4))),
        "adapter_up_weight": scatter_about(keys[3], (ADAPTER_TOTAL, ADAPTER_RANK, OUTPUT_FEATURES), ADAPTER_RANK ** -0.5, 0.75, ((0, 4), (2, 4))),
        "fetched_local_numbers": draw_fetched_local_numbers(jax.random.fold_in(jax.random.fold_in(keys[6], part), 71), part),
        "request_adapter_entry": draw_request_adapter_entry(jax.random.fold_in(jax.random.fold_in(keys[6], part), 71), part),
    }


adapter_scale = 0.5


def reference(attention_input, output_weight, adapter_down_weight, adapter_up_weight, fetched_local_numbers, request_adapter_entry):
    request_batch = attention_input.shape[0]
    group_of = jnp.arange(request_batch, dtype=jnp.int32) // REQ_DEV
    owner_of = request_adapter_entry // CAP
    adapter = ADP_DEV * owner_of + fetched_local_numbers[group_of, owner_of, request_adapter_entry % CAP]
    base_projected = jnp.dot(attention_input, output_weight, preferred_element_type=jnp.float32)
    grouped_blocks = attention_input.reshape(request_batch // 64, 64, QUERY_FEATURES)
    block_numbers = adapter.reshape(request_batch // 64, 64)

    def adapter_block(matched_pairs):
        block_rows, adapters_per_block = matched_pairs
        down_matrices = jnp.take(adapter_down_weight, adapters_per_block, axis=0).astype(jnp.float32)
        reduced_activation = jnp.einsum("nh,nhr->nr", block_rows.astype(jnp.float32), down_matrices, precision=lax.Precision.HIGHEST)
        up_matrices = jnp.take(adapter_up_weight, adapters_per_block, axis=0).astype(jnp.float32)
        return jnp.einsum("nr,nrd->nd", reduced_activation, up_matrices, precision=lax.Precision.HIGHEST)

    adapter_correction = lax.map(adapter_block, (grouped_blocks, block_numbers)).reshape(request_batch, OUTPUT_FEATURES)
    return (base_projected + adapter_scale * adapter_correction).astype(jnp.bfloat16)
```

```python
import functools

import jax
import jax.numpy as jnp
from jax import lax
from jax.experimental import pallas as pl
from jax.experimental.pallas import tpu as pltpu
from jax.sharding import PartitionSpec as P

adapter_scale = 0.5
CORES = 2


def kernel(
    sizes,
    entry_ref,
    fetched_ref,
    x_hbm,
    w_hbm,
    down_hbm,
    up_hbm,
    out_ref,
    x,
    w,
    downs,
    ups,
    part,
    core_in,
    x_in,
    shr,
    shr_in,
    aid,
    local_sem,
    w_sem,
    core_sem,
    xs_sem,
    shr_sem,
    zd_sem,
    yd_sem,
    zu_sem,
    yu_sem,
):
    reps, groups, tps, rank = sizes
    chips = tps // CORES
    rep = lax.axis_index("rep")
    me = lax.axis_index("dp")
    tp = lax.axis_index("tp")
    core = lax.rem(tp, CORES)
    chip = lax.div(tp, CORES)
    other_core = CORES * chip + (1 - core)
    other_rep = 1 - rep
    rows = x.shape[0]
    width = out_ref.shape[1]
    held = downs.shape[2]
    half = held // rank
    stored = half * reps
    cap = fetched_ref.shape[2]
    tile = w.shape[3]
    tiles = w.shape[1]
    f32 = jnp.float32

    def remote(src, dst, send, recv, target):
        return pltpu.make_async_remote_copy(
            src_ref=src,
            dst_ref=dst,
            send_sem=send,
            recv_sem=recv,
            device_id=target,
            device_id_type=pl.DeviceIdType.MESH,
        )

    load_x = pltpu.make_async_copy(x_hbm, x, local_sem.at[0])
    load_down = pltpu.make_async_copy(down_hbm, downs.at[me], local_sem.at[1])
    load_up = pltpu.make_async_copy(up_hbm, ups.at[me], local_sem.at[2])
    load_x.start()

    def column_of(j):
        far = lax.rem(chip + lax.div(j, 2) + 1, chips)
        return CORES * far + jnp.where(lax.rem(j, 2) == 0, 1 - core, core)

    def load_w(j, n):
        start = pl.multiple_of(column_of(j) * width + n * tile, 128)
        return pltpu.make_async_copy(
            w_hbm.at[:, pl.ds(start, tile)], w.at[j, n], w_sem.at[j, n]
        )

    @pl.loop(0, tps)
    def _(j):
        for n in range(tiles):
            load_w(j, n).start()

    load_down.start()
    load_up.start()

    barrier = pltpu.get_barrier_semaphore()

    def greet(target):
        pl.semaphore_signal(
            barrier, inc=1, device_id=target, device_id_type=pl.DeviceIdType.MESH
        )

    @pl.when(me > 0)
    def _():
        greet({"dp": me - 1})

    @pl.when(me < groups - 1)
    def _():
        greet({"dp": me + 1})

    greet({"rep": other_rep})

    @pl.loop(1, tps)
    def _(q):
        greet({"tp": lax.rem(tp + q, tps)})

    ends = jnp.where(me > 0, 1, 0) + jnp.where(me < groups - 1, 1, 0)
    pl.semaphore_wait(barrier, tps + ends)

    down_kind = (downs, down_hbm, zd_sem, yd_sem)
    up_kind = (ups, up_hbm, zu_sem, yu_sem)

    def piece(a):
        return pl.ds(a * rank, rank)

    def z_copy(kind, owner, a, side, own=False):
        buffer, source, z, _ = kind
        src = source.at[rep, piece(a)] if own else buffer.at[owner, rep, piece(a)]
        target = {"dp": me - 1} if side == 0 else {"dp": me + 1}
        return remote(
            src, buffer.at[owner, rep, piece(a)], z.at[side, owner, a], z.at[2, owner, a], target
        )

    def y_copy(kind, owner, a, mine):
        buffer, _, _, y = kind
        place = buffer.at[owner, rep if mine else other_rep, piece(a)]
        return remote(place, place, y.at[0, owner, a], y.at[1, owner, a], {"rep": other_rep})

    def send_own(kind, act):
        for a in range(half):

            @pl.when(me > 0)
            def _():
                act(z_copy(kind, me, a, 0, True))

            @pl.when(me < groups - 1)
            def _():
                act(z_copy(kind, me, a, 1, True))

    def relay(kind, k, a):
        @pl.when(me - k >= 0)
        def _():
            z_copy(kind, me - k, a, 1).wait_recv()

            @pl.when(me < groups - 1)
            def _():
                z_copy(kind, me - k, a, 1).start()

            y_copy(kind, me - k, a, True).start()

        @pl.when(me + k < groups)
        def _():
            z_copy(kind, me + k, a, 0).wait_recv()

            @pl.when(me > 0)
            def _():
                z_copy(kind, me + k, a, 0).start()

            y_copy(kind, me + k, a, True).start()

    def settle(kind, k, a):
        @pl.when(me - k >= 0)
        def _():
            @pl.when(me < groups - 1)
            def _():
                z_copy(kind, me - k, a, 1).wait_send()

            y_copy(kind, me - k, a, True).wait_send()

        @pl.when(me + k < groups)
        def _():
            @pl.when(me > 0)
            def _():
                z_copy(kind, me + k, a, 0).wait_send()

            y_copy(kind, me + k, a, True).wait_send()

    send_own(down_kind, lambda c: c.start())

    def core_copy(s):
        return remote(
            part.at[2 * s], core_in.at[s], core_sem.at[0, s], core_sem.at[1, s], {"tp": other_core}
        )

    def chip_copy(s):
        far = lax.rem(chip + s + 1, chips)
        return remote(
            part.at[2 * s + 1],
            x_in.at[s],
            xs_sem.at[0, s],
            xs_sem.at[1, s],
            {"tp": CORES * far + core},
        )

    load_x.wait()

    def multiply(j):
        @pl.loop(0, tiles)
        def _(n):
            load_w(j, n).wait()
            part[j, :, pl.ds(pl.multiple_of(n * tile, 128), tile)] = jnp.dot(
                x[...], w[j, n], preferred_element_type=f32
            )

    @pl.loop(0, chips)
    def _(s):
        multiply(2 * s)
        core_copy(s).start()

        @pl.when(s > 0)
        def _():
            core_copy(s - 1).wait_recv()
            part[2 * s - 1] = part[2 * s - 1] + core_in[s - 1]
            chip_copy(s - 1).start()

        multiply(2 * s + 1)

    aid[...] = jnp.zeros_like(aid)

    @pl.loop(0, groups)
    def _(o):
        entry = entry_ref[...]
        number = aid[...]
        for e in range(cap):
            number = jnp.where(entry == cap * o + e, stored * o + fetched_ref[me, o, e], number)
        aid[...] = number

    lane = lax.broadcasted_iota(jnp.int32, (rows, held), 1)
    lane_adapter = lax.div(lane, rank)

    def chosen(o, h):
        return aid[...] == stored * o + half * h + lane_adapter

    def shrink(o, h):
        product = lax.dot_general(
            x[...], downs[o, h], (((1,), (1,)), ((), ())), preferred_element_type=f32
        )
        shr[...] += jnp.where(chosen(o, h), product, 0.0)

    shr[...] = jnp.zeros_like(shr)
    load_down.wait()

    @pl.loop(0, reps)
    def _(h):
        shrink(me, h)

    @pl.loop(1, groups)
    def _(k):
        for a in range(half):
            relay(down_kind, k, a)

        @pl.when(me - k >= 0)
        def _():
            shrink(me - k, rep)

        @pl.when(me + k < groups)
        def _():
            shrink(me + k, rep)

    send_own(up_kind, lambda c: c.start())

    @pl.loop(0, groups)
    def _(o):
        @pl.when(o != me)
        def _():
            for a in range(half):
                y_copy(down_kind, o, a, False).wait_recv()
            shrink(o, other_rep)

    def shr_copy(q):
        return remote(
            shr,
            shr_in.at[q - 1],
            shr_sem.at[0, q - 1],
            shr_sem.at[1, q - 1],
            {"tp": lax.rem(tp + q, tps)},
        )

    @pl.loop(1, tps)
    def _(q):
        shr_copy(q).start()

    @pl.loop(1, groups)
    def _(k):
        for a in range(half):
            relay(up_kind, k, a)

    @pl.loop(1, tps)
    def _(q):
        shr_copy(q).wait()

    @pl.loop(1, tps)
    def _(q):
        shr[...] += shr_in[q - 1]

    base = part.at[tps - 1]
    core_copy(chips - 1).wait_recv()
    base[...] += core_in[chips - 1]

    @pl.loop(0, chips - 1)
    def _(s):
        chip_copy(s).wait_recv()
        base[...] += x_in[s]

    def expand(o, h):
        factor = jnp.where(chosen(o, h), adapter_scale * shr[...], 0.0)
        high = factor.astype(jnp.bfloat16)
        low = (factor - high.astype(f32)).astype(jnp.bfloat16)
        up = ups[o, h]
        base[...] += jnp.dot(high, up, preferred_element_type=f32) + jnp.dot(
            low, up, preferred_element_type=f32
        )

    load_up.wait()
    expand(me, other_rep)

    @pl.loop(0, groups)
    def _(o):
        expand(o, rep)

    @pl.loop(0, groups)
    def _(o):
        @pl.when(o != me)
        def _():
            for a in range(half):
                y_copy(up_kind, o, a, False).wait_recv()
            expand(o, other_rep)

    out_ref[...] = base[...].astype(out_ref.dtype)

    @pl.loop(0, chips)
    def _(s):
        core_copy(s).wait_send()

    @pl.loop(0, chips - 1)
    def _(s):
        chip_copy(s).wait_send()

    for kind in (down_kind, up_kind):
        send_own(kind, lambda c: c.wait_send())

        @pl.loop(1, groups)
        def _(k):
            for a in range(half):
                settle(kind, k, a)


def body(
    sizes,
    attention_input,
    output_weight,
    adapter_down_weight,
    adapter_up_weight,
    fetched_local_numbers,
    request_adapter_entry,
):
    reps, groups, tps = sizes
    chips = tps // CORES
    rows, features = attention_input.shape
    stored, _, rank = adapter_down_weight.shape
    width = adapter_up_weight.shape[2]
    half = stored // reps
    held = half * rank
    tile = min(512, width)
    tiles = width // tile
    down = adapter_down_weight.transpose(0, 2, 1).reshape(reps, held, features)
    up = adapter_up_weight.reshape(reps, held, width)
    entry = jnp.broadcast_to(request_adapter_entry[:, None], (rows, held))
    any_space = pl.BlockSpec(memory_space=pl.ANY)
    vmem = pl.BlockSpec(memory_space=pltpu.VMEM)
    dma = pltpu.SemaphoreType.DMA
    f32, bf16 = jnp.float32, jnp.bfloat16
    return pl.pallas_call(
        functools.partial(kernel, (reps, groups, tps, rank)),
        out_shape=jax.ShapeDtypeStruct((rows, width), bf16),
        in_specs=[vmem, pl.BlockSpec(memory_space=pltpu.SMEM)] + [any_space] * 4,
        out_specs=vmem,
        scratch_shapes=[
            pltpu.VMEM((rows, features), bf16),
            pltpu.VMEM((tps, tiles, features, tile), bf16),
            pltpu.VMEM((groups, reps, held, features), bf16),
            pltpu.VMEM((groups, reps, held, width), bf16),
            pltpu.VMEM((tps, rows, width), f32),
            pltpu.VMEM((chips, rows, width), f32),
            pltpu.VMEM((max(chips - 1, 1), rows, width), f32),
            pltpu.VMEM((rows, held), f32),
            pltpu.VMEM((tps - 1, rows, held), f32),
            pltpu.VMEM((rows, held), jnp.int32),
            dma((3,)),
            dma((tps, tiles)),
            dma((2, chips)),
            dma((2, max(chips - 1, 1))),
            dma((2, tps - 1)),
            dma((3, groups, half)),
            dma((2, groups, half)),
            dma((3, groups, half)),
            dma((2, groups, half)),
        ],
        compiler_params=pltpu.CompilerParams(
            collective_id=0, has_side_effects=True, vmem_limit_bytes=56 * 1024 * 1024
        ),
    )(entry, fetched_local_numbers, attention_input, output_weight, down, up)


def solution(mesh):
    in_specs = (
        P(("rep", "dp"), "tp"),
        P("tp", None),
        P("dp", "tp", None),
        P("dp", None, "tp"),
        P("rep", None, None),
        P(("rep", "dp")),
    )
    out_specs = P(("rep", "dp"), "tp")
    sizes = (mesh.shape["rep"], mesh.shape["dp"], mesh.shape["tp"])
    return jax.shard_map(
        functools.partial(body, sizes),
        mesh=mesh,
        in_specs=in_specs,
        out_specs=out_specs,
        check_vma=False,
    )
```

```python
import functools

import jax
import jax.numpy as jnp
from jax import lax
from jax.experimental import pallas as pl
from jax.experimental.pallas import tpu as pltpu
from jax.sharding import PartitionSpec as P

adapter_scale = 0.5
CORES = 2


def kernel(
    sizes,
    entry_ref,
    fetched_ref,
    x_hbm,
    w_hbm,
    down_hbm,
    up_hbm,
    out_ref,
    x,
    w,
    downs,
    ups,
    part,
    core_in,
    x_in,
    shr,
    shr_in,
    aid,
    place,
    row_out,
    row_in,
    code_out,
    code_in,
    ret_out,
    ret_in,
    local_sem,
    w_sem,
    core_sem,
    xs_sem,
    shr_sem,
    zd_sem,
    yd_sem,
    ed_sem,
    zu_sem,
    yu_sem,
    eu_sem,
    row_sem,
):
    reps, groups, tps, rank = sizes
    chips = tps // CORES
    rep = lax.axis_index("rep")
    me = lax.axis_index("dp")
    tp = lax.axis_index("tp")
    core = lax.rem(tp, CORES)
    chip = lax.div(tp, CORES)
    other_core = CORES * chip + (1 - core)
    other_rep = 1 - rep
    rows = x.shape[0]
    width = out_ref.shape[1]
    held = downs.shape[2]
    half = held // rank
    stored = half * reps
    cap = fetched_ref.shape[1]
    tiles, tile = w.shape[1], w.shape[3]
    last = groups - 1
    f32, bf16 = jnp.float32, jnp.bfloat16

    def remote(src, dst, send, recv, target):
        return pltpu.make_async_remote_copy(
            src_ref=src,
            dst_ref=dst,
            send_sem=send,
            recv_sem=recv,
            device_id=target,
            device_id_type=pl.DeviceIdType.MESH,
        )

    def start(c):
        c.start()

    def wait_send(c):
        c.wait_send()

    load_x = pltpu.make_async_copy(x_hbm, x, local_sem.at[0])
    load_down = pltpu.make_async_copy(down_hbm, downs.at[me], local_sem.at[1])
    load_up = pltpu.make_async_copy(up_hbm, ups.at[me], local_sem.at[2])
    load_x.start()

    def column_of(j):
        far = lax.rem(chip + lax.div(j, 2) + 1, chips)
        return CORES * far + jnp.where(lax.rem(j, 2) == 0, 1 - core, core)

    def load_w(j, n):
        first = pl.multiple_of(column_of(j) * width + n * tile, 128)
        return pltpu.make_async_copy(
            w_hbm.at[:, pl.ds(first, tile)], w.at[j, n], w_sem.at[j, n]
        )

    @pl.loop(0, tps)
    def _(j):
        for n in range(tiles):
            load_w(j, n).start()

    load_down.start()
    load_up.start()

    barrier = pltpu.get_barrier_semaphore()

    def greet(target):
        pl.semaphore_signal(
            barrier, inc=1, device_id=target, device_id_type=pl.DeviceIdType.MESH
        )

    @pl.when(me > 0)
    def _():
        greet({"dp": me - 1})

    @pl.when(me < last)
    def _():
        greet({"dp": me + 1})

    greet({"rep": other_rep})

    @pl.loop(1, tps)
    def _(q):
        greet({"tp": lax.rem(tp + q, tps)})

    edges = jnp.where(me > 0, 1, 0) + jnp.where(me < last, 1, 0)
    pl.semaphore_wait(barrier, tps + edges)

    down_kind = (downs, down_hbm, zd_sem, yd_sem, ed_sem)
    up_kind = (ups, up_hbm, zu_sem, yu_sem, eu_sem)
    at_end = (me == 0) | (me == last)
    serves = (me == 1) | (me == last - 1)
    step = (-1, 1)
    exists = (me > 0, me < last)
    next_inner = (me > 1, me < last - 1)

    def piece(a):
        return pl.ds(a * rank, rank)

    def z_copy(kind, owner, a, side, own=False):
        buffer, source, z = kind[:3]
        src = source.at[rep, piece(a)] if own else buffer.at[owner, rep, piece(a)]
        return remote(
            src,
            buffer.at[owner, rep, piece(a)],
            z.at[side, owner, a],
            z.at[2, owner, a],
            {"dp": me + step[side]},
        )

    def extra_copy(kind, owner, a, side):
        buffer, source, extra = kind[0], kind[1], kind[4]
        return remote(
            source.at[other_rep, piece(a)],
            buffer.at[owner, other_rep, piece(a)],
            extra.at[side, a],
            extra.at[3 - side, a],
            {"dp": me + step[side]},
        )

    def y_copy(kind, owner, a, mine):
        buffer, y = kind[0], kind[3]
        where = buffer.at[owner, rep if mine else other_rep, piece(a)]
        return remote(where, where, y.at[0, owner, a], y.at[1, owner, a], {"rep": other_rep})

    def own_to(kind, act, sides):
        for side in (0, 1):

            @pl.when(sides[side])
            def _():
                for a in range(half):
                    act(z_copy(kind, me, a, side, True))

    def extra_to(kind, act, sides):
        for side in (0, 1):

            @pl.when(sides[side])
            def _():
                for a in range(half):
                    act(extra_copy(kind, me, a, side))

    def each_owner(k, visit):
        for side in (0, 1):
            owner = me - step[side] * k

            @pl.when((owner >= 0) & (owner < groups))
            def _():
                visit(owner, side)

    def by_rows(k):
        return at_end & (k == 1)

    def by_extra(kind, owner, k):
        if kind is down_kind:
            return (k == 1) & ((owner == 0) | (owner == last))
        return (k == 1) & (owner > 0) & (owner < last) & (me > 0) & (me < last)

    def relay(kind, k, a, first):
        def visit(owner, side):
            def go():
                if first:
                    z_copy(kind, owner, a, side).wait_recv()

                @pl.when(exists[side])
                def _():
                    (start if first else wait_send)(z_copy(kind, owner, a, side))

                @pl.when(jnp.logical_not(by_extra(kind, owner, k)))
                def _():
                    (start if first else wait_send)(y_copy(kind, owner, a, True))

            if kind is down_kind:
                pl.when(jnp.logical_not(by_rows(k)))(go)
            else:
                go()

        each_owner(k, visit)

    def receive_other(kind, owner, side, k):
        extra = by_extra(kind, owner, k)

        @pl.when(extra)
        def _():
            for a in range(half):
                extra_copy(kind, owner, a, side).wait_recv()

        @pl.when(jnp.logical_not(extra))
        def _():
            for a in range(half):
                y_copy(kind, owner, a, False).wait_recv()

    down_first = next_inner
    up_first = (exists[0] & jnp.logical_not(next_inner[0]), exists[1] & jnp.logical_not(next_inner[1]))
    up_second = (next_inner[0] & jnp.logical_not(at_end), next_inner[1] & jnp.logical_not(at_end))
    up_third = (next_inner[0] & at_end, next_inner[1] & at_end)
    down_extra = (exists[0] & at_end, exists[1] & at_end)
    up_extra = up_second

    own_to(down_kind, start, down_first)
    own_to(up_kind, start, up_first)

    entry = jnp.broadcast_to(entry_ref[...].reshape(1, rows), (held, rows)).T
    aid[...] = jnp.zeros_like(aid)

    @pl.loop(0, groups)
    def _(o):
        number = aid[...]
        for e in range(cap):
            number = jnp.where(entry == cap * o + e, stored * o + fetched_ref[me, e, o], number)
        aid[...] = number

    lane = lax.broadcasted_iota(jnp.int32, (rows, held), 1)
    lane_adapter = lax.div(lane, rank)

    def chosen(o, h):
        return aid[...] == stored * o + half * h + lane_adapter

    load_x.wait()

    neighbour = jnp.where(me == 0, 1, last - 1)
    client = jnp.where(me == 1, 0, last)
    packed = row_out.shape[0]

    def row_copies():
        return (
            remote(row_out, row_in, row_sem.at[0], row_sem.at[1], {"dp": neighbour}),
            remote(code_out, code_in, row_sem.at[2], row_sem.at[3], {"dp": neighbour}),
        )

    ret_copy = remote(ret_out, ret_in, row_sem.at[4], row_sem.at[5], {"dp": client})

    @pl.when(at_end)
    def _():
        local = aid[...] - stored * neighbour
        uses = (local >= 0) & (local < stored)
        below = lax.broadcasted_iota(jnp.int32, (rows, rows), 1) < lax.broadcasted_iota(
            jnp.int32, (rows, rows), 0
        )
        order = jnp.dot(
            jnp.where(below, 1.0, 0.0).astype(bf16),
            jnp.where(uses, 1.0, 0.0).astype(bf16),
            preferred_element_type=f32,
        )
        spot = jnp.where(uses & (order == lane.astype(f32)), 1.0, 0.0)
        place[...] = spot.astype(bf16)
        pick = spot.T.astype(bf16)[:packed]
        row_out[...] = jnp.dot(pick, x[...], preferred_element_type=f32).astype(bf16)
        code_out[...] = jnp.dot(
            pick, local.astype(f32).astype(bf16), preferred_element_type=f32
        ).astype(bf16)
        for c in row_copies():
            c.start()

    def core_copy(s):
        return remote(
            part.at[2 * s], core_in.at[s], core_sem.at[0, s], core_sem.at[1, s], {"tp": other_core}
        )

    def chip_copy(s):
        far = lax.rem(chip + s + 1, chips)
        return remote(
            part.at[2 * s + 1],
            x_in.at[s],
            xs_sem.at[0, s],
            xs_sem.at[1, s],
            {"tp": CORES * far + core},
        )

    def multiply(j):
        @pl.loop(0, tiles)
        def _(n):
            load_w(j, n).wait()
            part[j, :, pl.ds(pl.multiple_of(n * tile, 128), tile)] = jnp.dot(
                x[...], w[j, n], preferred_element_type=f32
            )

    def pass_on(s):
        core_copy(s).wait_recv()
        part[2 * s + 1] = part[2 * s + 1] + core_in[s]
        chip_copy(s).start()

    @pl.loop(0, chips - 1)
    def _(s):
        multiply(2 * s)
        core_copy(s).start()

        @pl.when(s > 0)
        def _():
            pass_on(s - 1)

        multiply(2 * s + 1)

    pass_on(chips - 2)

    for a in range(half):
        relay(down_kind, 1, a, True)

    multiply(tps - 2)
    core_copy(chips - 1).start()
    multiply(tps - 1)

    def shrink(o, h):
        product = lax.dot_general(
            x[...], downs[o, h], (((1,), (1,)), ((), ())), preferred_element_type=f32
        )
        shr[...] += jnp.where(chosen(o, h), product, 0.0)

    shr[...] = jnp.zeros_like(shr)
    load_down.wait()

    def shrink_own(o, side):
        shrink(o, rep)

    @pl.loop(0, reps)
    def _(h):
        shrink(me, h)

    @pl.when(jnp.logical_not(at_end))
    def _():
        each_owner(1, shrink_own)

    for a in range(half):
        relay(down_kind, 2, a, True)
    own_to(up_kind, start, up_second)
    extra_to(down_kind, start, down_extra)
    each_owner(2, shrink_own)

    @pl.when(serves)
    def _():
        for c in row_copies():
            c.wait_recv()
        code = code_in[...].astype(f32).astype(jnp.int32)
        group = lax.div(lax.broadcasted_iota(jnp.int32, (packed, held), 1), rank)
        total = jnp.zeros((packed, held), f32)
        for h in range(reps):
            product = lax.dot_general(
                row_in[...], downs[me, h], (((1,), (1,)), ((), ())), preferred_element_type=f32
            )
            total = total + jnp.where(code == half * h + group, product, 0.0)
        ret_out[...] = total
        ret_copy.start()

    @pl.loop(3, groups)
    def _(k):
        for a in range(half):
            relay(down_kind, k, a, True)
        each_owner(k, shrink_own)

    own_to(up_kind, start, up_third)
    extra_to(up_kind, start, up_extra)

    for a in range(half):
        relay(up_kind, 1, a, True)

    @pl.loop(1, groups)
    def _(k):
        @pl.when(jnp.logical_not(by_rows(k)))
        def _():
            def visit(owner, side):
                receive_other(down_kind, owner, side, k)
                shrink(owner, other_rep)

            each_owner(k, visit)

    @pl.when(at_end)
    def _():
        ret_copy.wait_recv()
        rest = ret_in[...]
        spot = place[...][:, :packed]
        for _ in range(3):
            term = rest.astype(bf16)
            rest = rest - term.astype(f32)
            shr[...] += jnp.dot(spot, term, preferred_element_type=f32)

    def shr_copy(q):
        return remote(
            shr,
            shr_in.at[q - 1],
            shr_sem.at[0, q - 1],
            shr_sem.at[1, q - 1],
            {"tp": lax.rem(tp + q, tps)},
        )

    @pl.loop(1, tps)
    def _(q):
        shr_copy(q).start()

    for a in range(half):
        relay(up_kind, 2, a, True)

    base = part.at[tps - 1]
    core_copy(chips - 1).wait_recv()
    base[...] += core_in[chips - 1]

    @pl.loop(0, chips - 1)
    def _(s):
        chip_copy(s).wait_recv()
        base[...] += x_in[s]

    @pl.loop(3, groups)
    def _(k):
        for a in range(half):
            relay(up_kind, k, a, True)

    @pl.loop(1, tps)
    def _(q):
        shr_copy(q).wait()

    @pl.loop(1, tps)
    def _(q):
        shr[...] += shr_in[q - 1]

    def expand(o):
        factor = jnp.concatenate(
            [jnp.where(chosen(o, h), adapter_scale * shr[...], 0.0) for h in range(reps)], axis=1
        )
        high = factor.astype(bf16)
        low = (factor - high.astype(f32)).astype(bf16)
        up = ups[o].reshape(reps * held, width)
        base[...] += jnp.dot(high, up, preferred_element_type=f32) + jnp.dot(
            low, up, preferred_element_type=f32
        )

    load_up.wait()
    expand(me)

    @pl.loop(1, groups)
    def _(k):
        def visit(owner, side):
            receive_other(up_kind, owner, side, k)
            expand(owner)

        each_owner(k, visit)

    out_ref[...] = base[...].astype(out_ref.dtype)

    @pl.loop(0, chips)
    def _(s):
        core_copy(s).wait_send()

    @pl.loop(0, chips - 1)
    def _(s):
        chip_copy(s).wait_send()

    @pl.when(at_end)
    def _():
        for c in row_copies():
            c.wait_send()

    @pl.when(serves)
    def _():
        ret_copy.wait_send()

    own_to(down_kind, wait_send, down_first)
    extra_to(down_kind, wait_send, down_extra)
    own_to(up_kind, wait_send, exists)
    extra_to(up_kind, wait_send, up_extra)

    @pl.loop(1, groups)
    def _(k):
        for kind in (down_kind, up_kind):
            for a in range(half):
                relay(kind, k, a, False)


def body(
    sizes,
    attention_input,
    output_weight,
    adapter_down_weight,
    adapter_up_weight,
    fetched_local_numbers,
    request_adapter_entry,
):
    reps, groups, tps = sizes
    chips = tps // CORES
    rows, features = attention_input.shape
    stored, _, rank = adapter_down_weight.shape
    width = adapter_up_weight.shape[2]
    half = stored // reps
    held = half * rank
    tile = min(512, width)
    tiles = width // tile
    down = adapter_down_weight.transpose(0, 2, 1).reshape(reps, held, features)
    up = adapter_up_weight.reshape(reps, held, width)
    cap = fetched_local_numbers.shape[2]
    packed = rows * cap // groups
    any_space = pl.BlockSpec(memory_space=pl.ANY)
    vmem = pl.BlockSpec(memory_space=pltpu.VMEM)
    dma = pltpu.SemaphoreType.DMA
    f32, bf16 = jnp.float32, jnp.bfloat16
    return pl.pallas_call(
        functools.partial(kernel, (reps, groups, tps, rank)),
        out_shape=jax.ShapeDtypeStruct((rows, width), bf16),
        in_specs=[vmem, pl.BlockSpec(memory_space=pltpu.SMEM)] + [any_space] * 4,
        out_specs=vmem,
        scratch_shapes=[
            pltpu.VMEM((rows, features), bf16),
            pltpu.VMEM((tps, tiles, features, tile), bf16),
            pltpu.VMEM((groups, reps, held, features), bf16),
            pltpu.VMEM((groups, reps, held, width), bf16),
            pltpu.VMEM((tps, rows, width), f32),
            pltpu.VMEM((chips, rows, width), f32),
            pltpu.VMEM((max(chips - 1, 1), rows, width), f32),
            pltpu.VMEM((rows, held), f32),
            pltpu.VMEM((tps - 1, rows, held), f32),
            pltpu.VMEM((rows, held), jnp.int32),
            pltpu.VMEM((rows, held), bf16),
            pltpu.VMEM((packed, features), bf16),
            pltpu.VMEM((packed, features), bf16),
            pltpu.VMEM((packed, held), bf16),
            pltpu.VMEM((packed, held), bf16),
            pltpu.VMEM((packed, held), f32),
            pltpu.VMEM((packed, held), f32),
            dma((3,)),
            dma((tps, tiles)),
            dma((2, chips)),
            dma((2, max(chips - 1, 1))),
            dma((2, tps - 1)),
            dma((3, groups, half)),
            dma((2, groups, half)),
            dma((4, half)),
            dma((3, groups, half)),
            dma((2, groups, half)),
            dma((4, half)),
            dma((6,)),
        ],
        compiler_params=pltpu.CompilerParams(
            collective_id=0, has_side_effects=True, vmem_limit_bytes=56 * 1024 * 1024
        ),
    )(
        request_adapter_entry,
        fetched_local_numbers.transpose(0, 2, 1),
        attention_input,
        output_weight,
        down,
        up,
    )


def solution(mesh):
    in_specs = (
        P(("rep", "dp"), "tp"),
        P("tp", None),
        P("dp", "tp", None),
        P("dp", None, "tp"),
        P("rep", None, None),
        P(("rep", "dp")),
    )
    out_specs = P(("rep", "dp"), "tp")
    sizes = (mesh.shape["rep"], mesh.shape["dp"], mesh.shape["tp"])
    return jax.shard_map(
        functools.partial(body, sizes),
        mesh=mesh,
        in_specs=in_specs,
        out_specs=out_specs,
        check_vma=False,
    )
```

```python
import functools

import jax
import jax.numpy as jnp
from jax import lax
from jax.experimental import pallas as pl
from jax.experimental.pallas import tpu as pltpu
from jax.sharding import PartitionSpec as P

adapter_scale = 0.5
CORES = 2


def kernel(
    sizes,
    entry_ref,
    fetched_ref,
    x_hbm,
    w_hbm,
    down_hbm,
    up_hbm,
    out_ref,
    x,
    w,
    downs,
    ups,
    part,
    core_in,
    x_in,
    shr,
    shr_in,
    aid,
    place,
    row_out,
    row_in,
    code_out,
    code_in,
    ret_out,
    ret_in,
    local_sem,
    w_sem,
    core_sem,
    xs_sem,
    shr_sem,
    zd_sem,
    yd_sem,
    ed_sem,
    zu_sem,
    yu_sem,
    eu_sem,
    row_sem,
):
    reps, groups, tps, rank = sizes
    chips = tps // CORES
    rep = lax.axis_index("rep")
    me = lax.axis_index("dp")
    tp = lax.axis_index("tp")
    core = lax.rem(tp, CORES)
    chip = lax.div(tp, CORES)
    other_core = CORES * chip + (1 - core)
    other_rep = 1 - rep
    rows = x.shape[0]
    width = out_ref.shape[1]
    held = downs.shape[2]
    half = held // rank
    stored = half * reps
    cap = fetched_ref.shape[1]
    tiles, tile = w.shape[1], w.shape[3]
    last = groups - 1
    f32, bf16 = jnp.float32, jnp.bfloat16

    def remote(src, dst, send, recv, target):
        return pltpu.make_async_remote_copy(
            src_ref=src,
            dst_ref=dst,
            send_sem=send,
            recv_sem=recv,
            device_id=target,
            device_id_type=pl.DeviceIdType.MESH,
        )

    def start(c):
        c.start()

    def wait_send(c):
        c.wait_send()

    load_x = pltpu.make_async_copy(x_hbm, x, local_sem.at[0])
    load_down = pltpu.make_async_copy(down_hbm, downs.at[me], local_sem.at[1])
    load_up = pltpu.make_async_copy(up_hbm, ups.at[me], local_sem.at[2])
    load_x.start()

    def column_of(j):
        far = lax.rem(chip + lax.div(j, 2) + 1, chips)
        return CORES * far + jnp.where(lax.rem(j, 2) == 0, 1 - core, core)

    def load_w(j, n):
        first = pl.multiple_of(column_of(j) * width + n * tile, 128)
        return pltpu.make_async_copy(
            w_hbm.at[:, pl.ds(first, tile)], w.at[j, n], w_sem.at[j, n]
        )

    @pl.loop(0, tps)
    def _(j):
        for n in range(tiles):
            load_w(j, n).start()

    load_down.start()
    load_up.start()

    barrier = pltpu.get_barrier_semaphore()

    def greet(target):
        pl.semaphore_signal(
            barrier, inc=1, device_id=target, device_id_type=pl.DeviceIdType.MESH
        )

    @pl.when(me > 0)
    def _():
        greet({"dp": me - 1})

    @pl.when(me < last)
    def _():
        greet({"dp": me + 1})

    greet({"rep": other_rep})

    @pl.loop(1, tps)
    def _(q):
        greet({"tp": lax.rem(tp + q, tps)})

    edges = jnp.where(me > 0, 1, 0) + jnp.where(me < last, 1, 0)
    pl.semaphore_wait(barrier, tps + edges)

    down_kind = (downs, down_hbm, zd_sem, yd_sem, ed_sem)
    up_kind = (ups, up_hbm, zu_sem, yu_sem, eu_sem)
    at_end = (me == 0) | (me == last)
    serves = (me == 1) | (me == last - 1)
    step = (-1, 1)
    exists = (me > 0, me < last)
    next_inner = (me > 1, me < last - 1)

    def piece(a):
        return pl.ds(a * rank, rank)

    def z_copy(kind, owner, a, side, own=False):
        buffer, source, z = kind[:3]
        src = source.at[rep, piece(a)] if own else buffer.at[owner, rep, piece(a)]
        return remote(
            src,
            buffer.at[owner, rep, piece(a)],
            z.at[side, owner, a],
            z.at[2, owner, a],
            {"dp": me + step[side]},
        )

    def extra_copy(kind, owner, a, side):
        buffer, source, extra = kind[0], kind[1], kind[4]
        return remote(
            source.at[other_rep, piece(a)],
            buffer.at[owner, other_rep, piece(a)],
            extra.at[side, a],
            extra.at[3 - side, a],
            {"dp": me + step[side]},
        )

    def y_copy(kind, owner, a, mine):
        buffer, y = kind[0], kind[3]
        where = buffer.at[owner, rep if mine else other_rep, piece(a)]
        return remote(where, where, y.at[0, owner, a], y.at[1, owner, a], {"rep": other_rep})

    def own_to(kind, act, sides, pieces=range(half)):
        for side in (0, 1):

            @pl.when(sides[side])
            def _():
                for a in pieces:
                    act(z_copy(kind, me, a, side, True))

    def extra_to(kind, act, sides):
        for side in (0, 1):

            @pl.when(sides[side])
            def _():
                for a in extra_pieces(kind):
                    act(extra_copy(kind, me, a, side))

    def each_owner(k, visit):
        for side in (0, 1):
            owner = me - step[side] * k

            @pl.when((owner >= 0) & (owner < groups))
            def _():
                visit(owner, side)

    def by_rows(k):
        return at_end & (k == 1)

    def extra_pieces(kind):
        return range(max(half // 2, 1)) if kind is down_kind else range(half)

    def by_extra(kind, owner, k, a):
        if a not in extra_pieces(kind):
            return False
        if kind is down_kind:
            return (k == 1) & ((owner == 0) | (owner == last))
        return (k == 1) & (owner > 0) & (owner < last) & (me > 0) & (me < last)

    def relay(kind, k, a, first):
        def visit(owner, side):
            def go():
                if first:
                    z_copy(kind, owner, a, side).wait_recv()

                @pl.when(exists[side])
                def _():
                    (start if first else wait_send)(z_copy(kind, owner, a, side))

                @pl.when(jnp.logical_not(by_extra(kind, owner, k, a)))
                def _():
                    (start if first else wait_send)(y_copy(kind, owner, a, True))

            if kind is down_kind:
                pl.when(jnp.logical_not(by_rows(k)))(go)
            else:
                go()

        each_owner(k, visit)

    def receive_other(kind, owner, side, k):
        for a in range(half):
            extra = by_extra(kind, owner, k, a)

            @pl.when(extra)
            def _():
                extra_copy(kind, owner, a, side).wait_recv()

            @pl.when(jnp.logical_not(extra))
            def _():
                y_copy(kind, owner, a, False).wait_recv()

    down_first = next_inner
    up_first = (exists[0] & jnp.logical_not(next_inner[0]), exists[1] & jnp.logical_not(next_inner[1]))
    up_second = (next_inner[0] & jnp.logical_not(at_end), next_inner[1] & jnp.logical_not(at_end))
    up_third = (next_inner[0] & at_end, next_inner[1] & at_end)
    down_extra = (exists[0] & at_end, exists[1] & at_end)
    up_extra = up_second

    inner = jnp.logical_not(at_end)
    own_to(down_kind, start, down_first, range(1))
    own_to(up_kind, start, up_first)

    entry = jnp.broadcast_to(entry_ref[...].reshape(1, rows), (held, rows)).T
    aid[...] = jnp.zeros_like(aid)

    @pl.loop(0, groups)
    def _(o):
        number = aid[...]
        for e in range(cap):
            number = jnp.where(entry == cap * o + e, stored * o + fetched_ref[me, e, o], number)
        aid[...] = number

    lane = lax.broadcasted_iota(jnp.int32, (rows, held), 1)
    lane_adapter = lax.div(lane, rank)

    def chosen(o, h):
        return aid[...] == stored * o + half * h + lane_adapter

    load_x.wait()

    neighbour = jnp.where(me == 0, 1, last - 1)
    client = jnp.where(me == 1, 0, last)
    packed = row_out.shape[0]

    def row_copies():
        return (
            remote(row_out, row_in, row_sem.at[0], row_sem.at[1], {"dp": neighbour}),
            remote(code_out, code_in, row_sem.at[2], row_sem.at[3], {"dp": neighbour}),
        )

    ret_copy = remote(ret_out, ret_in, row_sem.at[4], row_sem.at[5], {"dp": client})

    def core_copy(s):
        return remote(
            part.at[2 * s], core_in.at[s], core_sem.at[0, s], core_sem.at[1, s], {"tp": other_core}
        )

    def chip_copy(s):
        far = lax.rem(chip + s + 1, chips)
        return remote(
            part.at[2 * s + 1],
            x_in.at[s],
            xs_sem.at[0, s],
            xs_sem.at[1, s],
            {"tp": CORES * far + core},
        )

    def multiply(j):
        @pl.loop(0, tiles)
        def _(n):
            load_w(j, n).wait()
            part[j, :, pl.ds(pl.multiple_of(n * tile, 128), tile)] = jnp.dot(
                x[...], w[j, n], preferred_element_type=f32
            )

    def pass_on(s):
        core_copy(s).wait_recv()
        part[2 * s + 1] = part[2 * s + 1] + core_in[s]
        chip_copy(s).start()

    @pl.loop(0, chips - 1)
    def _(s):
        multiply(2 * s)
        core_copy(s).start()

        @pl.when(s > 0)
        def _():
            pass_on(s - 1)

        multiply(2 * s + 1)

    own_to(down_kind, start, down_first, range(1, half))
    pass_on(chips - 2)

    @pl.when(inner)
    def _():
        relay(down_kind, 1, 0, True)

    multiply(tps - 2)
    core_copy(chips - 1).start()
    multiply(tps - 1)

    @pl.when(at_end)
    def _():
        local = aid[...] - stored * neighbour
        uses = (local >= 0) & (local < stored)
        below = lax.broadcasted_iota(jnp.int32, (rows, rows), 1) < lax.broadcasted_iota(
            jnp.int32, (rows, rows), 0
        )
        order = jnp.dot(
            jnp.where(below, 1.0, 0.0).astype(bf16),
            jnp.where(uses, 1.0, 0.0).astype(bf16),
            preferred_element_type=f32,
        )
        spot = jnp.where(uses & (order == lane.astype(f32)), 1.0, 0.0)
        place[...] = spot.astype(bf16)
        pick = spot.T.astype(bf16)[:packed]
        row_out[...] = jnp.dot(pick, x[...], preferred_element_type=f32).astype(bf16)
        code_out[...] = jnp.dot(
            pick, local.astype(f32).astype(bf16), preferred_element_type=f32
        ).astype(bf16)
        for c in row_copies():
            c.start()

    @pl.when(at_end)
    def _():
        for a in range(half):
            relay(up_kind, 1, a, True)

    @pl.when(inner)
    def _():
        for a in range(1, half):
            relay(down_kind, 1, a, True)

    def shrink(o, h):
        product = lax.dot_general(
            x[...], downs[o, h], (((1,), (1,)), ((), ())), preferred_element_type=f32
        )
        shr[...] += jnp.where(chosen(o, h), product, 0.0)

    shr[...] = jnp.zeros_like(shr)
    load_down.wait()

    def shrink_own(o, side):
        shrink(o, rep)

    @pl.loop(0, reps)
    def _(h):
        shrink(me, h)

    @pl.when(inner)
    def _():
        each_owner(1, shrink_own)

    relay(down_kind, 2, 0, True)
    own_to(up_kind, start, up_second)
    for a in range(1, half):
        relay(down_kind, 2, a, True)
    own_to(up_kind, start, up_third)
    each_owner(2, shrink_own)

    @pl.when(serves)
    def _():
        for c in row_copies():
            c.wait_recv()
        code = code_in[...].astype(f32).astype(jnp.int32)
        group = lax.div(lax.broadcasted_iota(jnp.int32, (packed, held), 1), rank)
        total = jnp.zeros((packed, held), f32)
        for h in range(reps):
            product = lax.dot_general(
                row_in[...], downs[me, h], (((1,), (1,)), ((), ())), preferred_element_type=f32
            )
            total = total + jnp.where(code == half * h + group, product, 0.0)
        ret_out[...] = total
        ret_copy.start()

    @pl.loop(3, groups)
    def _(k):
        for a in range(half):
            relay(down_kind, k, a, True)
            if a == 0:

                @pl.when(k == 3)
                def _():
                    extra_to(down_kind, start, down_extra)

        each_owner(k, shrink_own)

    def shrink_other(k, wanted):
        def visit(owner, side):
            def go():
                receive_other(down_kind, owner, side, k)
                shrink(owner, other_rep)

            pl.when(wanted(owner))(go)

        each_owner(k, visit)

    def from_end(owner):
        return (owner == 0) | (owner == last)

    @pl.when(inner)
    def _():
        shrink_other(1, lambda owner: jnp.logical_not(from_end(owner)))
        for a in range(half):
            relay(up_kind, 1, a, True)

    extra_to(up_kind, start, up_extra)

    @pl.when(at_end)
    def _():
        shrink_other(2, lambda owner: True)
        ret_copy.wait_recv()
        rest = ret_in[...]
        spot = place[...][:, :packed]
        for _ in range(3):
            term = rest.astype(bf16)
            rest = rest - term.astype(f32)
            shr[...] += jnp.dot(spot, term, preferred_element_type=f32)

    for a in range(half):
        relay(up_kind, 2, a, True)

    @pl.when(inner)
    def _():
        shrink_other(2, lambda owner: True)
        shrink_other(1, from_end)

    @pl.loop(3, groups)
    def _(k):
        shrink_other(k, lambda owner: True)

    def shr_copy(q):
        return remote(
            shr,
            shr_in.at[q - 1],
            shr_sem.at[0, q - 1],
            shr_sem.at[1, q - 1],
            {"tp": lax.rem(tp + q, tps)},
        )

    @pl.loop(1, tps)
    def _(q):
        shr_copy(q).start()

    base = part.at[tps - 1]
    core_copy(chips - 1).wait_recv()
    base[...] += core_in[chips - 1]

    @pl.loop(0, chips - 1)
    def _(s):
        chip_copy(s).wait_recv()
        base[...] += x_in[s]

    @pl.loop(3, groups)
    def _(k):
        for a in range(half):
            relay(up_kind, k, a, True)

    @pl.loop(1, tps)
    def _(q):
        shr_copy(q).wait()

    @pl.loop(1, tps)
    def _(q):
        shr[...] += shr_in[q - 1]

    def expand(o):
        factor = jnp.concatenate(
            [jnp.where(chosen(o, h), adapter_scale * shr[...], 0.0) for h in range(reps)], axis=1
        )
        high = factor.astype(bf16)
        low = (factor - high.astype(f32)).astype(bf16)
        up = ups[o].reshape(reps * held, width)
        base[...] += jnp.dot(high, up, preferred_element_type=f32) + jnp.dot(
            low, up, preferred_element_type=f32
        )

    load_up.wait()
    expand(me)

    @pl.loop(1, groups)
    def _(k):
        def visit(owner, side):
            receive_other(up_kind, owner, side, k)
            expand(owner)

        each_owner(k, visit)

    out_ref[...] = base[...].astype(out_ref.dtype)

    @pl.loop(0, chips)
    def _(s):
        core_copy(s).wait_send()

    @pl.loop(0, chips - 1)
    def _(s):
        chip_copy(s).wait_send()

    @pl.when(at_end)
    def _():
        for c in row_copies():
            c.wait_send()

    @pl.when(serves)
    def _():
        ret_copy.wait_send()

    own_to(down_kind, wait_send, down_first)
    extra_to(down_kind, wait_send, down_extra)
    own_to(up_kind, wait_send, exists)
    extra_to(up_kind, wait_send, up_extra)

    @pl.loop(1, groups)
    def _(k):
        for kind in (down_kind, up_kind):
            for a in range(half):
                relay(kind, k, a, False)


def body(
    sizes,
    attention_input,
    output_weight,
    adapter_down_weight,
    adapter_up_weight,
    fetched_local_numbers,
    request_adapter_entry,
):
    reps, groups, tps = sizes
    chips = tps // CORES
    rows, features = attention_input.shape
    stored, _, rank = adapter_down_weight.shape
    width = adapter_up_weight.shape[2]
    half = stored // reps
    held = half * rank
    tile = min(512, width)
    tiles = width // tile
    down = adapter_down_weight.transpose(0, 2, 1).reshape(reps, held, features)
    up = adapter_up_weight.reshape(reps, held, width)
    cap = fetched_local_numbers.shape[2]
    packed = rows * cap // groups
    any_space = pl.BlockSpec(memory_space=pl.ANY)
    vmem = pl.BlockSpec(memory_space=pltpu.VMEM)
    dma = pltpu.SemaphoreType.DMA
    f32, bf16 = jnp.float32, jnp.bfloat16
    return pl.pallas_call(
        functools.partial(kernel, (reps, groups, tps, rank)),
        out_shape=jax.ShapeDtypeStruct((rows, width), bf16),
        in_specs=[vmem, pl.BlockSpec(memory_space=pltpu.SMEM)] + [any_space] * 4,
        out_specs=vmem,
        scratch_shapes=[
            pltpu.VMEM((rows, features), bf16),
            pltpu.VMEM((tps, tiles, features, tile), bf16),
            pltpu.VMEM((groups, reps, held, features), bf16),
            pltpu.VMEM((groups, reps, held, width), bf16),
            pltpu.VMEM((tps, rows, width), f32),
            pltpu.VMEM((chips, rows, width), f32),
            pltpu.VMEM((max(chips - 1, 1), rows, width), f32),
            pltpu.VMEM((rows, held), f32),
            pltpu.VMEM((tps - 1, rows, held), f32),
            pltpu.VMEM((rows, held), jnp.int32),
            pltpu.VMEM((rows, held), bf16),
            pltpu.VMEM((packed, features), bf16),
            pltpu.VMEM((packed, features), bf16),
            pltpu.VMEM((packed, held), bf16),
            pltpu.VMEM((packed, held), bf16),
            pltpu.VMEM((packed, held), f32),
            pltpu.VMEM((packed, held), f32),
            dma((3,)),
            dma((tps, tiles)),
            dma((2, chips)),
            dma((2, max(chips - 1, 1))),
            dma((2, tps - 1)),
            dma((3, groups, half)),
            dma((2, groups, half)),
            dma((4, half)),
            dma((3, groups, half)),
            dma((2, groups, half)),
            dma((4, half)),
            dma((6,)),
        ],
        compiler_params=pltpu.CompilerParams(
            collective_id=0, has_side_effects=True, vmem_limit_bytes=56 * 1024 * 1024
        ),
    )(
        request_adapter_entry,
        fetched_local_numbers.transpose(0, 2, 1),
        attention_input,
        output_weight,
        down,
        up,
    )


def solution(mesh):
    in_specs = (
        P(("rep", "dp"), "tp"),
        P("tp", None),
        P("dp", "tp", None),
        P("dp", None, "tp"),
        P("rep", None, None),
        P(("rep", "dp")),
    )
    out_specs = P(("rep", "dp"), "tp")
    sizes = (mesh.shape["rep"], mesh.shape["dp"], mesh.shape["tp"])
    return jax.shard_map(
        functools.partial(body, sizes),
        mesh=mesh,
        in_specs=in_specs,
        out_specs=out_specs,
        check_vma=False,
    )
```

```python
import functools

import jax
import jax.numpy as jnp
from jax import lax
from jax.experimental import pallas as pl
from jax.experimental.pallas import tpu as pltpu
from jax.sharding import PartitionSpec as P

adapter_scale = 0.5
CORES = 2


def kernel(
    sizes,
    entry_ref,
    fetched_ref,
    x_hbm,
    w_hbm,
    down_hbm,
    up_hbm,
    out_ref,
    x,
    w,
    downs,
    ups,
    part,
    core_in,
    x_in,
    shr,
    shr_own,
    shr_core,
    shr_pair,
    shr_in,
    picked,
    aid,
    place,
    row_out,
    row_in,
    code_out,
    code_in,
    ret_out,
    ret_in,
    local_sem,
    w_sem,
    core_sem,
    xs_sem,
    shr_sem,
    zd_sem,
    yd_sem,
    ed_sem,
    zu_sem,
    yu_sem,
    eu_sem,
    row_sem,
):
    reps, groups, tps, rank = sizes
    chips = tps // CORES
    rep = lax.axis_index("rep")
    me = lax.axis_index("dp")
    tp = lax.axis_index("tp")
    core = lax.rem(tp, CORES)
    chip = lax.div(tp, CORES)
    other_core = CORES * chip + (1 - core)
    other_rep = 1 - rep
    rows = x.shape[0]
    width = out_ref.shape[1]
    held = downs.shape[2]
    half = held // rank
    stored = half * reps
    cap = fetched_ref.shape[1]
    tiles, tile = w.shape[1], w.shape[3]
    last = groups - 1
    f32, bf16 = jnp.float32, jnp.bfloat16

    def remote(src, dst, send, recv, target):
        return pltpu.make_async_remote_copy(
            src_ref=src,
            dst_ref=dst,
            send_sem=send,
            recv_sem=recv,
            device_id=target,
            device_id_type=pl.DeviceIdType.MESH,
        )

    def start(c):
        c.start()

    def wait_send(c):
        c.wait_send()

    load_x = pltpu.make_async_copy(x_hbm, x, local_sem.at[0])
    load_down = pltpu.make_async_copy(down_hbm, downs.at[me], local_sem.at[1])
    load_up = pltpu.make_async_copy(up_hbm, ups.at[me], local_sem.at[2])
    load_x.start()
    load_up.start()

    def column_of(j):
        far = lax.rem(chip + lax.div(j, 2) + 1, chips)
        return CORES * far + jnp.where(lax.rem(j, 2) == 0, 1 - core, core)

    def load_w(j, n):
        first = pl.multiple_of(column_of(j) * width + n * tile, 128)
        return pltpu.make_async_copy(
            w_hbm.at[:, pl.ds(first, tile)], w.at[j, n], w_sem.at[j, n]
        )

    @pl.loop(0, tps)
    def _(j):
        for n in range(tiles):
            load_w(j, n).start()

    load_down.start()

    barrier = pltpu.get_barrier_semaphore()

    def greet(target):
        pl.semaphore_signal(
            barrier, inc=1, device_id=target, device_id_type=pl.DeviceIdType.MESH
        )

    @pl.when(me > 0)
    def _():
        greet({"dp": me - 1})

    @pl.when(me < last)
    def _():
        greet({"dp": me + 1})

    greet({"rep": other_rep})

    @pl.loop(1, tps)
    def _(q):
        greet({"tp": lax.rem(tp + q, tps)})

    edges = jnp.where(me > 0, 1, 0) + jnp.where(me < last, 1, 0)
    pl.semaphore_wait(barrier, tps + edges)

    down_kind = (downs, down_hbm, zd_sem, yd_sem, ed_sem)
    up_kind = (ups, up_hbm, zu_sem, yu_sem, eu_sem)
    at_end = (me == 0) | (me == last)
    serves = (me == 1) | (me == last - 1)
    step = (-1, 1)
    exists = (me > 0, me < last)
    next_inner = (me > 1, me < last - 1)

    def piece(a):
        return pl.ds(a * rank, rank)

    def z_copy(kind, owner, a, side, source=None):
        buffer, _, z = kind[:3]
        src = buffer.at[owner, rep, piece(a)] if source is None else source.at[piece(a)]
        return remote(
            src,
            buffer.at[owner, rep, piece(a)],
            z.at[side, owner, a],
            z.at[2, owner, a],
            {"dp": me + step[side]},
        )

    def extra_copy(kind, owner, a, side):
        buffer, source, extra = kind[0], kind[1], kind[4]
        return remote(
            source.at[other_rep, piece(a)],
            buffer.at[owner, other_rep, piece(a)],
            extra.at[side, a],
            extra.at[3 - side, a],
            {"dp": me + step[side]},
        )

    def y_copy(kind, owner, a, mine):
        buffer, y = kind[0], kind[3]
        where = buffer.at[owner, rep if mine else other_rep, piece(a)]
        return remote(where, where, y.at[0, owner, a], y.at[1, owner, a], {"rep": other_rep})

    def own_to(kind, act, sides, pieces=range(half), source=None):
        for side in (0, 1):

            @pl.when(sides[side])
            def _():
                for a in pieces:
                    act(z_copy(kind, me, a, side, kind[1].at[rep] if source is None else source))

    def extra_to(kind, act, sides):
        for side in (0, 1):

            @pl.when(sides[side])
            def _():
                for a in extra_pieces(kind):
                    act(extra_copy(kind, me, a, side))

    def each_owner(k, visit):
        for side in (0, 1):
            owner = me - step[side] * k

            @pl.when((owner >= 0) & (owner < groups))
            def _():
                visit(owner, side)

    def by_rows(k):
        return at_end & (k == 1)

    def extra_pieces(kind):
        return range(max(half // 2, 1)) if kind is down_kind else range(half)

    def by_extra(kind, owner, k, a):
        if a not in extra_pieces(kind):
            return False
        if kind is down_kind:
            return (k == 1) & ((owner == 0) | (owner == last))
        return (k == 1) & (me > 0) & (me < last)

    def relay(kind, k, a, first):
        def visit(owner, side):
            def go():
                if first:
                    z_copy(kind, owner, a, side).wait_recv()

                @pl.when(exists[side])
                def _():
                    (start if first else wait_send)(z_copy(kind, owner, a, side))

                @pl.when(jnp.logical_not(by_extra(kind, owner, k, a) | by_rows(k)))
                def _():
                    (start if first else wait_send)(y_copy(kind, owner, a, True))

            if kind is down_kind:
                pl.when(jnp.logical_not(by_rows(k)))(go)
            else:
                go()

        each_owner(k, visit)

    def receive_other(kind, owner, side, k):
        for a in range(half):
            extra = by_extra(kind, owner, k, a)

            @pl.when(extra)
            def _():
                extra_copy(kind, owner, a, side).wait_recv()

            @pl.when(jnp.logical_not(extra))
            def _():
                y_copy(kind, owner, a, False).wait_recv()

    down_first = next_inner
    up_first = (exists[0] & jnp.logical_not(next_inner[0]), exists[1] & jnp.logical_not(next_inner[1]))
    up_second = (next_inner[0] & jnp.logical_not(at_end), next_inner[1] & jnp.logical_not(at_end))
    up_third = (next_inner[0] & at_end, next_inner[1] & at_end)
    down_extra = (exists[0] & at_end, exists[1] & at_end)
    up_extra = next_inner

    inner = jnp.logical_not(at_end)
    own_to(down_kind, start, down_first, range(1))

    neighbour = jnp.where(me == 0, 1, last - 1)
    client = jnp.where(me == 1, 0, last)
    load_up.wait()

    @pl.when(serves)
    def _():
        for e in range(cap):
            number = fetched_ref[client, e, me]
            value = ups[me, 0, piece(0)]
            for j in range(1, stored):
                value = jnp.where(number == j, ups[me, j // half, piece(j % half)], value)
            picked[piece(e)] = value

    own_to(up_kind, start, up_first, source=picked)

    entry = jnp.broadcast_to(entry_ref[...].reshape(1, rows), (held, rows)).T
    aid[...] = jnp.zeros_like(aid)

    @pl.loop(0, groups)
    def _(o):
        number = aid[...]
        for e in range(cap):
            number = jnp.where(entry == cap * o + e, stored * o + fetched_ref[me, e, o], number)
        aid[...] = number

    lane = lax.broadcasted_iota(jnp.int32, (rows, held), 1)
    lane_adapter = lax.div(lane, rank)

    def chosen(o, h):
        return aid[...] == stored * o + half * h + lane_adapter

    load_x.wait()

    packed = row_out.shape[0]

    def row_copies():
        return (
            remote(row_out, row_in, row_sem.at[0], row_sem.at[1], {"dp": neighbour}),
            remote(code_out, code_in, row_sem.at[2], row_sem.at[3], {"dp": neighbour}),
        )

    ret_copy = remote(ret_out, ret_in, row_sem.at[4], row_sem.at[5], {"dp": client})

    def core_copy(s):
        return remote(
            part.at[2 * s], core_in.at[s], core_sem.at[0, s], core_sem.at[1, s], {"tp": other_core}
        )

    def chip_copy(s):
        far = lax.rem(chip + s + 1, chips)
        return remote(
            part.at[2 * s + 1],
            x_in.at[s],
            xs_sem.at[0, s],
            xs_sem.at[1, s],
            {"tp": CORES * far + core},
        )

    def multiply(j):
        @pl.loop(0, tiles)
        def _(n):
            load_w(j, n).wait()
            part[j, :, pl.ds(pl.multiple_of(n * tile, 128), tile)] = jnp.dot(
                x[...], w[j, n], preferred_element_type=f32
            )

    def pass_on(s):
        core_copy(s).wait_recv()
        part[2 * s + 1] = part[2 * s + 1] + core_in[s]
        chip_copy(s).start()

    @pl.loop(0, chips - 1)
    def _(s):
        multiply(2 * s)
        core_copy(s).start()

        @pl.when(s > 0)
        def _():
            pass_on(s - 1)

        multiply(2 * s + 1)

    own_to(down_kind, start, down_first, range(1, half))
    pass_on(chips - 2)

    @pl.when(inner)
    def _():
        relay(down_kind, 1, 0, True)

    multiply(tps - 2)
    core_copy(chips - 1).start()
    multiply(tps - 1)

    @pl.when(at_end)
    def _():
        local = aid[...] - stored * neighbour
        uses = (local >= 0) & (local < stored)
        below = lax.broadcasted_iota(jnp.int32, (rows, rows), 1) < lax.broadcasted_iota(
            jnp.int32, (rows, rows), 0
        )
        order = jnp.dot(
            jnp.where(below, 1.0, 0.0).astype(bf16),
            jnp.where(uses, 1.0, 0.0).astype(bf16),
            preferred_element_type=f32,
        )
        spot = jnp.where(uses & (order == lane.astype(f32)), 1.0, 0.0)
        place[...] = spot.astype(bf16)
        pick = spot.T.astype(bf16)[:packed]
        row_out[...] = jnp.dot(pick, x[...], preferred_element_type=f32).astype(bf16)
        code_out[...] = jnp.dot(
            pick, local.astype(f32).astype(bf16), preferred_element_type=f32
        ).astype(bf16)
        for c in row_copies():
            c.start()

    @pl.when(at_end)
    def _():
        for a in range(half):
            relay(up_kind, 1, a, True)

    @pl.when(inner)
    def _():
        for a in range(1, half):
            relay(down_kind, 1, a, True)

    def shrink(o, h):
        product = lax.dot_general(
            x[...], downs[o, h], (((1,), (1,)), ((), ())), preferred_element_type=f32
        )
        shr[...] += jnp.where(chosen(o, h), product, 0.0)

    shr[...] = jnp.zeros_like(shr)
    load_down.wait()

    def shrink_own(o, side):
        shrink(o, rep)

    @pl.loop(0, reps)
    def _(h):
        shrink(me, h)

    @pl.when(inner)
    def _():
        each_owner(1, shrink_own)

    relay(down_kind, 2, 0, True)
    own_to(up_kind, start, up_second)
    for a in range(1, half):
        relay(down_kind, 2, a, True)
    own_to(up_kind, start, up_third)
    each_owner(2, shrink_own)

    @pl.when(serves)
    def _():
        for c in row_copies():
            c.wait_recv()
        code = code_in[...].astype(f32).astype(jnp.int32)
        group = lax.div(lax.broadcasted_iota(jnp.int32, (packed, held), 1), rank)
        total = jnp.zeros((packed, held), f32)
        for h in range(reps):
            product = lax.dot_general(
                row_in[...], downs[me, h], (((1,), (1,)), ((), ())), preferred_element_type=f32
            )
            total = total + jnp.where(code == half * h + group, product, 0.0)
        ret_out[...] = total
        ret_copy.start()

    @pl.loop(3, groups)
    def _(k):
        for a in range(half):
            relay(down_kind, k, a, True)
            if a == 0:

                @pl.when(k == 3)
                def _():
                    extra_to(down_kind, start, down_extra)

        each_owner(k, shrink_own)

    def shrink_other(k, wanted):
        def visit(owner, side):
            def go():
                receive_other(down_kind, owner, side, k)
                shrink(owner, other_rep)

            pl.when(wanted(owner))(go)

        each_owner(k, visit)

    def from_end(owner):
        return (owner == 0) | (owner == last)

    @pl.when(inner)
    def _():
        shrink_other(1, lambda owner: jnp.logical_not(from_end(owner)))
        for a in range(half):
            relay(up_kind, 1, a, True)

    extra_to(up_kind, start, up_extra)

    @pl.when(at_end)
    def _():
        shrink_other(2, lambda owner: True)
        ret_copy.wait_recv()
        rest = ret_in[...]
        spot = place[...][:, :packed]
        for _ in range(3):
            term = rest.astype(bf16)
            rest = rest - term.astype(f32)
            shr[...] += jnp.dot(spot, term, preferred_element_type=f32)

    for a in range(half):
        relay(up_kind, 2, a, True)

    @pl.when(inner)
    def _():
        shrink_other(2, lambda owner: True)
        shrink_other(1, from_end)

    @pl.loop(3, groups)
    def _(k):
        shrink_other(k, lambda owner: True)

    block = rows // half
    lane_group = lane_adapter[:block]

    def spread(value):
        total = value
        for g in range(1, half):
            total = total + pltpu.roll(value, g * rank, 1)
        return total

    whole = spread(shr[...])
    pack = jnp.zeros((block, held), f32)
    for g in range(half):
        pack = jnp.where(lane_group == g, whole[g * block : (g + 1) * block], pack)
    shr_own[...] = pack

    shr_core_copy = remote(
        shr_own, shr_core, shr_sem.at[0, chips - 1], shr_sem.at[1, chips - 1], {"tp": other_core}
    )

    def shr_copy(s):
        far = lax.rem(chip + s + 1, chips)
        return remote(
            shr_pair,
            shr_in.at[s],
            shr_sem.at[0, s],
            shr_sem.at[1, s],
            {"tp": CORES * far + core},
        )

    shr_core_copy.start()
    base = part.at[tps - 1]
    core_copy(chips - 1).wait_recv()
    base[...] += core_in[chips - 1]
    shr_core_copy.wait_recv()
    shr_pair[...] = shr_own[...] + shr_core[...]

    @pl.loop(0, chips - 1)
    def _(s):
        shr_copy(s).start()

    @pl.loop(0, chips - 1)
    def _(s):
        chip_copy(s).wait_recv()
        base[...] += x_in[s]

    @pl.loop(3, groups)
    def _(k):
        for a in range(half):
            relay(up_kind, k, a, True)

    shr_own_sum = shr_pair[...]
    for s in range(chips - 1):
        shr_copy(s).wait_recv()
        shr_own_sum = shr_own_sum + shr_in[s]
    for g in range(half):
        shr[g * block : (g + 1) * block] = spread(jnp.where(lane_group == g, shr_own_sum, 0.0))

    def expand(o):
        masks = [chosen(o, h) for h in range(reps)]
        expand_by(masks, ups[o].reshape(reps * held, width))

    def expand_by(masks, up):
        factor = jnp.concatenate(
            [jnp.where(mask, adapter_scale * shr[...], 0.0) for mask in masks], axis=1
        )
        high = factor.astype(bf16)
        low = (factor - high.astype(f32)).astype(bf16)
        base[...] += jnp.dot(high, up, preferred_element_type=f32) + jnp.dot(
            low, up, preferred_element_type=f32
        )

    expand(me)

    @pl.when(at_end)
    def _():
        number = jnp.zeros((rows, held), jnp.int32)
        for e in range(cap):
            number = jnp.where(lane_adapter == e, fetched_ref[me, e, neighbour], number)
        expand_by([aid[...] == stored * neighbour + number], ups[neighbour, rep])

    @pl.when(inner)
    def _():
        def visit(owner, side):
            receive_other(up_kind, owner, side, 1)
            expand(owner)

        each_owner(1, visit)

    @pl.loop(2, groups)
    def _(k):
        def visit(owner, side):
            receive_other(up_kind, owner, side, k)
            expand(owner)

        each_owner(k, visit)

    out_ref[...] = base[...].astype(out_ref.dtype)

    @pl.loop(0, chips)
    def _(s):
        core_copy(s).wait_send()

    @pl.loop(0, chips - 1)
    def _(s):
        chip_copy(s).wait_send()

    @pl.when(at_end)
    def _():
        for c in row_copies():
            c.wait_send()

    @pl.when(serves)
    def _():
        ret_copy.wait_send()

    own_to(down_kind, wait_send, down_first)
    extra_to(down_kind, wait_send, down_extra)
    own_to(up_kind, wait_send, up_first, source=picked)
    own_to(up_kind, wait_send, up_second)
    own_to(up_kind, wait_send, up_third)
    shr_core_copy.wait_send()

    @pl.loop(0, chips - 1)
    def _(s):
        shr_copy(s).wait_send()

    extra_to(up_kind, wait_send, up_extra)

    @pl.loop(1, groups)
    def _(k):
        for kind in (down_kind, up_kind):
            for a in range(half):
                relay(kind, k, a, False)


def body(
    sizes,
    attention_input,
    output_weight,
    adapter_down_weight,
    adapter_up_weight,
    fetched_local_numbers,
    request_adapter_entry,
):
    reps, groups, tps = sizes
    chips = tps // CORES
    rows, features = attention_input.shape
    stored, _, rank = adapter_down_weight.shape
    width = adapter_up_weight.shape[2]
    half = stored // reps
    held = half * rank
    tile = min(512, width)
    tiles = width // tile
    down = adapter_down_weight.transpose(0, 2, 1).reshape(reps, held, features)
    up = adapter_up_weight.reshape(reps, held, width)
    cap = fetched_local_numbers.shape[2]
    packed = rows * cap // groups
    any_space = pl.BlockSpec(memory_space=pl.ANY)
    vmem = pl.BlockSpec(memory_space=pltpu.VMEM)
    dma = pltpu.SemaphoreType.DMA
    f32, bf16 = jnp.float32, jnp.bfloat16
    return pl.pallas_call(
        functools.partial(kernel, (reps, groups, tps, rank)),
        out_shape=jax.ShapeDtypeStruct((rows, width), bf16),
        in_specs=[vmem, pl.BlockSpec(memory_space=pltpu.SMEM)] + [any_space] * 4,
        out_specs=vmem,
        scratch_shapes=[
            pltpu.VMEM((rows, features), bf16),
            pltpu.VMEM((tps, tiles, features, tile), bf16),
            pltpu.VMEM((groups, reps, held, features), bf16),
            pltpu.VMEM((groups, reps, held, width), bf16),
            pltpu.VMEM((tps, rows, width), f32),
            pltpu.VMEM((chips, rows, width), f32),
            pltpu.VMEM((chips - 1, rows, width), f32),
            pltpu.VMEM((rows, held), f32),
            pltpu.VMEM((rows // half, held), f32),
            pltpu.VMEM((rows // half, held), f32),
            pltpu.VMEM((rows // half, held), f32),
            pltpu.VMEM((chips - 1, rows // half, held), f32),
            pltpu.VMEM((held, width), bf16),
            pltpu.VMEM((rows, held), jnp.int32),
            pltpu.VMEM((rows, held), bf16),
            pltpu.VMEM((packed, features), bf16),
            pltpu.VMEM((packed, features), bf16),
            pltpu.VMEM((packed, held), bf16),
            pltpu.VMEM((packed, held), bf16),
            pltpu.VMEM((packed, held), f32),
            pltpu.VMEM((packed, held), f32),
            dma((3,)),
            dma((tps, tiles)),
            dma((2, chips)),
            dma((2, chips - 1)),
            dma((2, chips)),
            dma((3, groups, half)),
            dma((2, groups, half)),
            dma((4, half)),
            dma((3, groups, half)),
            dma((2, groups, half)),
            dma((4, half)),
            dma((6,)),
        ],
        compiler_params=pltpu.CompilerParams(
            collective_id=0, has_side_effects=True, vmem_limit_bytes=56 * 1024 * 1024
        ),
    )(
        request_adapter_entry,
        fetched_local_numbers.transpose(0, 2, 1),
        attention_input,
        output_weight,
        down,
        up,
    )


def solution(mesh):
    in_specs = (
        P(("rep", "dp"), "tp"),
        P("tp", None),
        P("dp", "tp", None),
        P("dp", None, "tp"),
        P("rep", None, None),
        P(("rep", "dp")),
    )
    out_specs = P(("rep", "dp"), "tp")
    sizes = (mesh.shape["rep"], mesh.shape["dp"], mesh.shape["tp"])
    return jax.shard_map(
        functools.partial(body, sizes),
        mesh=mesh,
        in_specs=in_specs,
        out_specs=out_specs,
        check_vma=False,
    )
```

```python
import functools

import jax
import jax.numpy as jnp
from jax import lax
from jax.experimental import pallas as pl
from jax.experimental.pallas import tpu as pltpu
from jax.sharding import PartitionSpec as P

adapter_scale = 0.5
CORES = 2


def kernel(
    sizes,
    entry_ref,
    fetched_ref,
    x_hbm,
    w_hbm,
    down_hbm,
    up_hbm,
    out_ref,
    x,
    w,
    downs,
    ups,
    part,
    core_in,
    x_in,
    shr,
    shr_own,
    shr_core,
    shr_pair,
    shr_in,
    picked,
    aid,
    place,
    row_out,
    row_in,
    code_out,
    code_in,
    ret_out,
    ret_in,
    local_sem,
    w_sem,
    core_sem,
    xs_sem,
    shr_sem,
    zd_sem,
    yd_sem,
    ed_sem,
    zu_sem,
    yu_sem,
    eu_sem,
    row_sem,
):
    reps, groups, tps, rank = sizes
    chips = tps // CORES
    rep = lax.axis_index("rep")
    me = lax.axis_index("dp")
    tp = lax.axis_index("tp")
    core = lax.rem(tp, CORES)
    chip = lax.div(tp, CORES)
    other_core = CORES * chip + (1 - core)
    other_rep = 1 - rep
    rows = x.shape[0]
    width = out_ref.shape[1]
    held = downs.shape[2]
    half = held // rank
    stored = half * reps
    cap = fetched_ref.shape[1]
    tiles, tile = w.shape[1], w.shape[3]
    last = groups - 1
    f32, bf16 = jnp.float32, jnp.bfloat16

    def remote(src, dst, send, recv, target):
        return pltpu.make_async_remote_copy(
            src_ref=src,
            dst_ref=dst,
            send_sem=send,
            recv_sem=recv,
            device_id=target,
            device_id_type=pl.DeviceIdType.MESH,
        )

    def start(c):
        c.start()

    def wait_send(c):
        c.wait_send()

    load_x = pltpu.make_async_copy(x_hbm, x, local_sem.at[0])
    load_down = pltpu.make_async_copy(down_hbm, downs.at[me], local_sem.at[1])
    load_up = pltpu.make_async_copy(up_hbm, ups.at[me], local_sem.at[2])
    load_x.start()
    load_up.start()

    def column_of(j):
        far = lax.rem(chip + lax.div(j, 2) + 1, chips)
        return CORES * far + jnp.where(lax.rem(j, 2) == 0, 1 - core, core)

    def load_w(j, n):
        first = pl.multiple_of(column_of(j) * width + n * tile, 128)
        return pltpu.make_async_copy(
            w_hbm.at[:, pl.ds(first, tile)], w.at[j, n], w_sem.at[j, n]
        )

    @pl.loop(0, tps)
    def _(j):
        for n in range(tiles):
            load_w(j, n).start()

    load_down.start()

    barrier = pltpu.get_barrier_semaphore()

    def greet(target):
        pl.semaphore_signal(
            barrier, inc=1, device_id=target, device_id_type=pl.DeviceIdType.MESH
        )

    @pl.when(me > 0)
    def _():
        greet({"dp": me - 1})

    @pl.when(me < last)
    def _():
        greet({"dp": me + 1})

    greet({"rep": other_rep})

    @pl.loop(1, tps)
    def _(q):
        greet({"tp": lax.rem(tp + q, tps)})

    edges = jnp.where(me > 0, 1, 0) + jnp.where(me < last, 1, 0)
    pl.semaphore_wait(barrier, tps + edges)

    down_kind = (downs, down_hbm, zd_sem, yd_sem, ed_sem)
    up_kind = (ups, up_hbm, zu_sem, yu_sem, eu_sem)
    at_end = (me == 0) | (me == last)
    serves = (me == 1) | (me == last - 1)
    step = (-1, 1)
    exists = (me > 0, me < last)
    next_inner = (me > 1, me < last - 1)

    def piece(a):
        return pl.ds(a * rank, rank)

    def z_copy(kind, owner, a, side, source=None):
        buffer, _, z = kind[:3]
        src = buffer.at[owner, rep, piece(a)] if source is None else source.at[piece(a)]
        return remote(
            src,
            buffer.at[owner, rep, piece(a)],
            z.at[side, owner, a],
            z.at[2, owner, a],
            {"dp": me + step[side]},
        )

    def extra_copy(kind, owner, a, side):
        buffer, source, extra = kind[0], kind[1], kind[4]
        return remote(
            source.at[other_rep, piece(a)],
            buffer.at[owner, other_rep, piece(a)],
            extra.at[side, a],
            extra.at[3 - side, a],
            {"dp": me + step[side]},
        )

    def y_copy(kind, owner, a, mine):
        buffer, y = kind[0], kind[3]
        where = buffer.at[owner, rep if mine else other_rep, piece(a)]
        return remote(where, where, y.at[0, owner, a], y.at[1, owner, a], {"rep": other_rep})

    def own_to(kind, act, sides, pieces=range(half), source=None):
        for side in (0, 1):

            @pl.when(sides[side])
            def _():
                for a in pieces:
                    act(z_copy(kind, me, a, side, kind[1].at[rep] if source is None else source))

    def extra_to(kind, act, sides):
        for side in (0, 1):

            @pl.when(sides[side])
            def _():
                for a in extra_pieces(kind):
                    act(extra_copy(kind, me, a, side))

    def each_owner(k, visit):
        for side in (0, 1):
            owner = me - step[side] * k

            @pl.when((owner >= 0) & (owner < groups))
            def _():
                visit(owner, side)

    def by_rows(k):
        return at_end & (k == 1)

    def extra_pieces(kind):
        return range(max(half // 2, 1)) if kind is down_kind else range(half)

    def by_extra(kind, owner, k, a):
        if a not in extra_pieces(kind):
            return False
        if kind is down_kind:
            return (k == 1) & ((owner == 0) | (owner == last))
        return (k == 1) & (me > 0) & (me < last)

    def from_end(owner):
        return (owner == 0) | (owner == last)

    def not_from_end(owner):
        return jnp.logical_not(from_end(owner))

    def relay(kind, k, a, first, wanted=None):
        def visit(owner, side):
            def go():
                if first:
                    z_copy(kind, owner, a, side).wait_recv()

                @pl.when(exists[side])
                def _():
                    (start if first else wait_send)(z_copy(kind, owner, a, side))

                @pl.when(jnp.logical_not(by_extra(kind, owner, k, a) | by_rows(k)))
                def _():
                    (start if first else wait_send)(y_copy(kind, owner, a, True))

            if wanted is not None:
                pl.when(wanted(owner))(go)
            elif kind is down_kind:
                pl.when(jnp.logical_not(by_rows(k)))(go)
            else:
                go()

        each_owner(k, visit)

    def receive_other(kind, owner, side, k):
        for a in range(half):
            extra = by_extra(kind, owner, k, a)

            @pl.when(extra)
            def _():
                extra_copy(kind, owner, a, side).wait_recv()

            @pl.when(jnp.logical_not(extra))
            def _():
                y_copy(kind, owner, a, False).wait_recv()

    down_first = next_inner
    up_first = (exists[0] & jnp.logical_not(next_inner[0]), exists[1] & jnp.logical_not(next_inner[1]))
    up_second = (next_inner[0] & jnp.logical_not(at_end), next_inner[1] & jnp.logical_not(at_end))
    up_third = (next_inner[0] & at_end, next_inner[1] & at_end)
    down_extra = (exists[0] & at_end, exists[1] & at_end)
    up_extra = next_inner

    inner = jnp.logical_not(at_end)
    own_to(down_kind, start, down_first, range(1))

    neighbour = jnp.where(me == 0, 1, last - 1)
    client = jnp.where(me == 1, 0, last)
    load_up.wait()

    @pl.when(serves)
    def _():
        for e in range(cap):
            number = fetched_ref[client, e, me]
            value = ups[me, 0, piece(0)]
            for j in range(1, stored):
                value = jnp.where(number == j, ups[me, j // half, piece(j % half)], value)
            picked[piece(e)] = value

    own_to(up_kind, start, up_first, source=picked)

    entry = jnp.broadcast_to(entry_ref[...].reshape(1, rows), (held, rows)).T
    aid[...] = jnp.zeros_like(aid)

    @pl.loop(0, groups)
    def _(o):
        number = aid[...]
        for e in range(cap):
            number = jnp.where(entry == cap * o + e, stored * o + fetched_ref[me, e, o], number)
        aid[...] = number

    lane = lax.broadcasted_iota(jnp.int32, (rows, held), 1)
    lane_adapter = lax.div(lane, rank)

    def chosen(o, h):
        return aid[...] == stored * o + half * h + lane_adapter

    load_x.wait()

    packed = row_out.shape[0]

    def row_copies():
        return (
            remote(row_out, row_in, row_sem.at[0], row_sem.at[1], {"dp": neighbour}),
            remote(code_out, code_in, row_sem.at[2], row_sem.at[3], {"dp": neighbour}),
        )

    ret_copy = remote(ret_out, ret_in, row_sem.at[4], row_sem.at[5], {"dp": client})

    def core_copy(s):
        return remote(
            part.at[2 * s], core_in.at[s], core_sem.at[0, s], core_sem.at[1, s], {"tp": other_core}
        )

    def chip_copy(s):
        far = lax.rem(chip + s + 1, chips)
        return remote(
            part.at[2 * s + 1],
            x_in.at[s],
            xs_sem.at[0, s],
            xs_sem.at[1, s],
            {"tp": CORES * far + core},
        )

    def multiply(j):
        @pl.loop(0, tiles)
        def _(n):
            load_w(j, n).wait()
            part[j, :, pl.ds(pl.multiple_of(n * tile, 128), tile)] = jnp.dot(
                x[...], w[j, n], preferred_element_type=f32
            )

    def pass_on(s):
        core_copy(s).wait_recv()
        part[2 * s + 1] = part[2 * s + 1] + core_in[s]
        chip_copy(s).start()

    @pl.loop(0, chips - 1)
    def _(s):
        multiply(2 * s)
        core_copy(s).start()

        @pl.when(s > 0)
        def _():
            pass_on(s - 1)

        multiply(2 * s + 1)

    pass_on(chips - 2)
    own_to(down_kind, start, down_first, range(1, half))

    @pl.when(inner)
    def _():
        relay(down_kind, 1, 0, True)

    own_to(up_kind, start, up_third)
    multiply(tps - 2)
    core_copy(chips - 1).start()
    multiply(tps - 1)

    @pl.when(at_end)
    def _():
        local = aid[...] - stored * neighbour
        uses = (local >= 0) & (local < stored)
        below = lax.broadcasted_iota(jnp.int32, (rows, rows), 1) < lax.broadcasted_iota(
            jnp.int32, (rows, rows), 0
        )
        order = jnp.dot(
            jnp.where(below, 1.0, 0.0).astype(bf16),
            jnp.where(uses, 1.0, 0.0).astype(bf16),
            preferred_element_type=f32,
        )
        spot = jnp.where(uses & (order == lane.astype(f32)), 1.0, 0.0)
        place[...] = spot.astype(bf16)
        pick = spot.T.astype(bf16)[:packed]
        row_out[...] = jnp.dot(pick, x[...], preferred_element_type=f32).astype(bf16)
        code_out[...] = jnp.dot(
            pick, local.astype(f32).astype(bf16), preferred_element_type=f32
        ).astype(bf16)
        for c in row_copies():
            c.start()

    @pl.when(at_end)
    def _():
        for a in range(half):
            relay(up_kind, 1, a, True)

    @pl.when(inner)
    def _():
        for a in range(1, half):
            relay(down_kind, 1, a, True)

    def shrink(o, h):
        product = lax.dot_general(
            x[...], downs[o, h], (((1,), (1,)), ((), ())), preferred_element_type=f32
        )
        shr[...] += jnp.where(chosen(o, h), product, 0.0)

    shr[...] = jnp.zeros_like(shr)
    load_down.wait()

    def shrink_own(o, side):
        shrink(o, rep)

    @pl.loop(0, reps)
    def _(h):
        shrink(me, h)

    @pl.when(inner)
    def _():
        each_owner(1, shrink_own)

    relay(down_kind, 2, 0, True)
    own_to(up_kind, start, up_second)
    for a in range(1, half):
        relay(down_kind, 2, a, True)

    @pl.when(inner)
    def _():
        for a in range(half):
            relay(up_kind, 1, a, True, from_end)

    each_owner(2, shrink_own)

    @pl.loop(3, groups)
    def _(k):
        for a in range(half):
            relay(down_kind, k, a, True)
            if a == 0:

                @pl.when(k == 3)
                def _():
                    extra_to(down_kind, start, down_extra)

        each_owner(k, shrink_own)

    def shrink_other(k, wanted):
        def visit(owner, side):
            def go():
                receive_other(down_kind, owner, side, k)
                shrink(owner, other_rep)

            pl.when(wanted(owner))(go)

        each_owner(k, visit)

    @pl.when(inner)
    def _():
        shrink_other(1, not_from_end)
        for a in range(half):
            relay(up_kind, 1, a, True, not_from_end)

    @pl.when(serves)
    def _():
        for c in row_copies():
            c.wait_recv()
        code = code_in[...].astype(f32).astype(jnp.int32)
        group = lax.div(lax.broadcasted_iota(jnp.int32, (packed, held), 1), rank)
        total = jnp.zeros((packed, held), f32)
        for h in range(reps):
            product = lax.dot_general(
                row_in[...], downs[me, h], (((1,), (1,)), ((), ())), preferred_element_type=f32
            )
            total = total + jnp.where(code == half * h + group, product, 0.0)
        ret_out[...] = total
        ret_copy.start()

    extra_to(up_kind, start, up_extra)

    @pl.when(at_end)
    def _():
        shrink_other(2, lambda owner: True)
        ret_copy.wait_recv()
        rest = ret_in[...]
        spot = place[...][:, :packed]
        for _ in range(3):
            term = rest.astype(bf16)
            rest = rest - term.astype(f32)
            shr[...] += jnp.dot(spot, term, preferred_element_type=f32)

    for a in range(half):
        relay(up_kind, 2, a, True)

    @pl.when(inner)
    def _():
        shrink_other(2, lambda owner: True)
        shrink_other(1, from_end)

    @pl.loop(3, groups)
    def _(k):
        shrink_other(k, lambda owner: True)

    block = rows // half
    lane_group = lane_adapter[:block]

    def spread(value):
        total = value
        for g in range(1, half):
            total = total + pltpu.roll(value, g * rank, 1)
        return total

    whole = spread(shr[...])
    pack = jnp.zeros((block, held), f32)
    for g in range(half):
        pack = jnp.where(lane_group == g, whole[g * block : (g + 1) * block], pack)
    shr_own[...] = pack

    shr_core_copy = remote(
        shr_own, shr_core, shr_sem.at[0, chips - 1], shr_sem.at[1, chips - 1], {"tp": other_core}
    )

    def shr_copy(s):
        far = lax.rem(chip + s + 1, chips)
        return remote(
            shr_pair,
            shr_in.at[s],
            shr_sem.at[0, s],
            shr_sem.at[1, s],
            {"tp": CORES * far + core},
        )

    shr_core_copy.start()
    base = part.at[tps - 1]
    core_copy(chips - 1).wait_recv()
    base[...] += core_in[chips - 1]
    shr_core_copy.wait_recv()
    shr_pair[...] = shr_own[...] + shr_core[...]

    @pl.loop(0, chips - 1)
    def _(s):
        shr_copy(s).start()

    @pl.loop(0, chips - 1)
    def _(s):
        chip_copy(s).wait_recv()
        base[...] += x_in[s]

    @pl.loop(3, groups)
    def _(k):
        for a in range(half):
            relay(up_kind, k, a, True)

    shr_own_sum = shr_pair[...]
    for s in range(chips - 1):
        shr_copy(s).wait_recv()
        shr_own_sum = shr_own_sum + shr_in[s]
    for g in range(half):
        shr[g * block : (g + 1) * block] = spread(jnp.where(lane_group == g, shr_own_sum, 0.0))

    def expand(o):
        masks = [chosen(o, h) for h in range(reps)]
        expand_by(masks, ups[o].reshape(reps * held, width))

    def expand_by(masks, up):
        factor = jnp.concatenate(
            [jnp.where(mask, adapter_scale * shr[...], 0.0) for mask in masks], axis=1
        )
        high = factor.astype(bf16)
        low = (factor - high.astype(f32)).astype(bf16)
        base[...] += jnp.dot(high, up, preferred_element_type=f32) + jnp.dot(
            low, up, preferred_element_type=f32
        )

    expand(me)

    @pl.when(at_end)
    def _():
        number = jnp.zeros((rows, held), jnp.int32)
        for e in range(cap):
            number = jnp.where(lane_adapter == e, fetched_ref[me, e, neighbour], number)
        expand_by([aid[...] == stored * neighbour + number], ups[neighbour, rep])

    @pl.when(inner)
    def _():
        def visit(owner, side):
            receive_other(up_kind, owner, side, 1)
            expand(owner)

        each_owner(1, visit)

    @pl.loop(2, groups)
    def _(k):
        def visit(owner, side):
            receive_other(up_kind, owner, side, k)
            expand(owner)

        each_owner(k, visit)

    out_ref[...] = base[...].astype(out_ref.dtype)

    @pl.loop(0, chips)
    def _(s):
        core_copy(s).wait_send()

    @pl.loop(0, chips - 1)
    def _(s):
        chip_copy(s).wait_send()

    @pl.when(at_end)
    def _():
        for c in row_copies():
            c.wait_send()

    @pl.when(serves)
    def _():
        ret_copy.wait_send()

    own_to(down_kind, wait_send, down_first)
    extra_to(down_kind, wait_send, down_extra)
    own_to(up_kind, wait_send, up_first, source=picked)
    own_to(up_kind, wait_send, up_second)
    own_to(up_kind, wait_send, up_third)
    shr_core_copy.wait_send()

    @pl.loop(0, chips - 1)
    def _(s):
        shr_copy(s).wait_send()

    extra_to(up_kind, wait_send, up_extra)

    @pl.loop(1, groups)
    def _(k):
        for kind in (down_kind, up_kind):
            for a in range(half):
                relay(kind, k, a, False)


def body(
    sizes,
    attention_input,
    output_weight,
    adapter_down_weight,
    adapter_up_weight,
    fetched_local_numbers,
    request_adapter_entry,
):
    reps, groups, tps = sizes
    chips = tps // CORES
    rows, features = attention_input.shape
    stored, _, rank = adapter_down_weight.shape
    width = adapter_up_weight.shape[2]
    half = stored // reps
    held = half * rank
    tile = min(512, width)
    tiles = width // tile
    down = adapter_down_weight.transpose(0, 2, 1).reshape(reps, held, features)
    up = adapter_up_weight.reshape(reps, held, width)
    cap = fetched_local_numbers.shape[2]
    packed = rows * cap // groups
    any_space = pl.BlockSpec(memory_space=pl.ANY)
    vmem = pl.BlockSpec(memory_space=pltpu.VMEM)
    dma = pltpu.SemaphoreType.DMA
    f32, bf16 = jnp.float32, jnp.bfloat16
    return pl.pallas_call(
        functools.partial(kernel, (reps, groups, tps, rank)),
        out_shape=pltpu.VMEM((rows, width), bf16),
        in_specs=[vmem, pl.BlockSpec(memory_space=pltpu.SMEM)] + [any_space] * 4,
        out_specs=vmem,
        scratch_shapes=[
            pltpu.VMEM((rows, features), bf16),
            pltpu.VMEM((tps, tiles, features, tile), bf16),
            pltpu.VMEM((groups, reps, held, features), bf16),
            pltpu.VMEM((groups, reps, held, width), bf16),
            pltpu.VMEM((tps, rows, width), f32),
            pltpu.VMEM((chips, rows, width), f32),
            pltpu.VMEM((chips - 1, rows, width), f32),
            pltpu.VMEM((rows, held), f32),
            pltpu.VMEM((rows // half, held), f32),
            pltpu.VMEM((rows // half, held), f32),
            pltpu.VMEM((rows // half, held), f32),
            pltpu.VMEM((chips - 1, rows // half, held), f32),
            pltpu.VMEM((held, width), bf16),
            pltpu.VMEM((rows, held), jnp.int32),
            pltpu.VMEM((rows, held), bf16),
            pltpu.VMEM((packed, features), bf16),
            pltpu.VMEM((packed, features), bf16),
            pltpu.VMEM((packed, held), bf16),
            pltpu.VMEM((packed, held), bf16),
            pltpu.VMEM((packed, held), f32),
            pltpu.VMEM((packed, held), f32),
            dma((3,)),
            dma((tps, tiles)),
            dma((2, chips)),
            dma((2, chips - 1)),
            dma((2, chips)),
            dma((3, groups, half)),
            dma((2, groups, half)),
            dma((4, half)),
            dma((3, groups, half)),
            dma((2, groups, half)),
            dma((4, half)),
            dma((6,)),
        ],
        compiler_params=pltpu.CompilerParams(
            collective_id=0, has_side_effects=True, vmem_limit_bytes=56 * 1024 * 1024
        ),
    )(
        request_adapter_entry,
        fetched_local_numbers.transpose(0, 2, 1),
        attention_input,
        output_weight,
        down,
        up,
    )


def solution(mesh):
    in_specs = (
        P(("rep", "dp"), "tp"),
        P("tp", None),
        P("dp", "tp", None),
        P("dp", None, "tp"),
        P("rep", None, None),
        P(("rep", "dp")),
    )
    out_specs = P(("rep", "dp"), "tp")
    sizes = (mesh.shape["rep"], mesh.shape["dp"], mesh.shape["tp"])
    return jax.shard_map(
        functools.partial(body, sizes),
        mesh=mesh,
        in_specs=in_specs,
        out_specs=out_specs,
        check_vma=False,
    )
```

```python
import functools

import jax
import jax.numpy as jnp
from jax import lax
from jax.experimental import pallas as pl
from jax.experimental.pallas import tpu as pltpu
from jax.sharding import PartitionSpec as P

adapter_scale = 0.5
CORES = 2


def kernel(
    sizes,
    entry_ref,
    fetched_ref,
    x_hbm,
    w_hbm,
    down_hbm,
    up_hbm,
    out_ref,
    x,
    w,
    downs,
    ups,
    part,
    core_in,
    x_in,
    shr,
    shr_own,
    shr_core,
    shr_pair,
    shr_in,
    picked,
    aid,
    place,
    row_out,
    row_in,
    code_out,
    code_in,
    ret_out,
    ret_in,
    local_sem,
    w_sem,
    core_sem,
    xs_sem,
    shr_sem,
    zd_sem,
    yd_sem,
    ed_sem,
    zu_sem,
    yu_sem,
    eu_sem,
    row_sem,
):
    reps, groups, tps, rank = sizes
    chips = tps // CORES
    rep = lax.axis_index("rep")
    me = lax.axis_index("dp")
    tp = lax.axis_index("tp")
    core = lax.rem(tp, CORES)
    chip = lax.div(tp, CORES)
    other_core = CORES * chip + (1 - core)
    other_rep = 1 - rep
    rows = x.shape[0]
    width = out_ref.shape[1]
    held = downs.shape[2]
    half = held // rank
    stored = half * reps
    cap = fetched_ref.shape[1]
    tiles, tile = w.shape[1], w.shape[3]
    last = groups - 1
    f32, bf16 = jnp.float32, jnp.bfloat16

    def remote(src, dst, send, recv, target):
        return pltpu.make_async_remote_copy(
            src_ref=src,
            dst_ref=dst,
            send_sem=send,
            recv_sem=recv,
            device_id=target,
            device_id_type=pl.DeviceIdType.MESH,
        )

    def start(c):
        c.start()

    def wait_send(c):
        c.wait_send()

    load_x = pltpu.make_async_copy(x_hbm, x, local_sem.at[0])
    load_down = pltpu.make_async_copy(down_hbm, downs.at[me], local_sem.at[1])
    load_up = pltpu.make_async_copy(up_hbm, ups.at[me], local_sem.at[2])
    load_x.start()
    load_up.start()

    def column_of(j):
        far = lax.rem(chip + lax.div(j, 2) + 1, chips)
        return CORES * far + jnp.where(lax.rem(j, 2) == 0, 1 - core, core)

    def load_w(j, n):
        first = pl.multiple_of(column_of(j) * width + n * tile, 128)
        return pltpu.make_async_copy(
            w_hbm.at[:, pl.ds(first, tile)], w.at[j, n], w_sem.at[j, n]
        )

    @pl.loop(0, tps)
    def _(j):
        for n in range(tiles):
            load_w(j, n).start()

    load_down.start()

    barrier = pltpu.get_barrier_semaphore()

    def greet(target):
        pl.semaphore_signal(
            barrier, inc=1, device_id=target, device_id_type=pl.DeviceIdType.MESH
        )

    @pl.when(me > 0)
    def _():
        greet({"dp": me - 1})

    @pl.when(me < last)
    def _():
        greet({"dp": me + 1})

    greet({"rep": other_rep})

    @pl.loop(1, tps)
    def _(q):
        greet({"tp": lax.rem(tp + q, tps)})

    edges = jnp.where(me > 0, 1, 0) + jnp.where(me < last, 1, 0)
    pl.semaphore_wait(barrier, tps + edges)

    down_kind = (downs, down_hbm, zd_sem, yd_sem, ed_sem)
    up_kind = (ups, up_hbm, zu_sem, yu_sem, eu_sem)
    at_end = (me == 0) | (me == last)
    serves = (me == 1) | (me == last - 1)
    step = (-1, 1)
    exists = (me > 0, me < last)
    next_inner = (me > 1, me < last - 1)

    def piece(a):
        return pl.ds(a * rank, rank)

    def z_copy(kind, owner, a, side, source=None):
        buffer, _, z = kind[:3]
        src = buffer.at[owner, rep, piece(a)] if source is None else source.at[piece(a)]
        return remote(
            src,
            buffer.at[owner, rep, piece(a)],
            z.at[side, owner, a],
            z.at[2, owner, a],
            {"dp": me + step[side]},
        )

    def extra_copy(kind, owner, a, side):
        buffer, source, extra = kind[0], kind[1], kind[4]
        return remote(
            source.at[other_rep, piece(a)],
            buffer.at[owner, other_rep, piece(a)],
            extra.at[side, a],
            extra.at[3 - side, a],
            {"dp": me + step[side]},
        )

    def y_copy(kind, owner, a, mine):
        buffer, y = kind[0], kind[3]
        where = buffer.at[owner, rep if mine else other_rep, piece(a)]
        return remote(where, where, y.at[0, owner, a], y.at[1, owner, a], {"rep": other_rep})

    def own_to(kind, act, sides, pieces=range(half), source=None):
        for side in (0, 1):

            @pl.when(sides[side])
            def _():
                for a in pieces:
                    act(z_copy(kind, me, a, side, kind[1].at[rep] if source is None else source))

    def extra_to(kind, act, sides):
        for side in (0, 1):

            @pl.when(sides[side])
            def _():
                for a in extra_pieces(kind):
                    act(extra_copy(kind, me, a, side))

    def each_owner(k, visit):
        for side in (0, 1):
            owner = me - step[side] * k

            @pl.when((owner >= 0) & (owner < groups))
            def _():
                visit(owner, side)

    def by_rows(k):
        return at_end & (k == 1)

    def extra_pieces(kind):
        return range(max(half // 2, 1)) if kind is down_kind else range(half)

    def by_extra(kind, owner, k, a):
        if a not in extra_pieces(kind):
            return False
        if kind is down_kind:
            return (k == 1) & ((owner == 0) | (owner == last))
        return (k == 1) & (me > 0) & (me < last)

    def from_end(owner):
        return (owner == 0) | (owner == last)

    def not_from_end(owner):
        return jnp.logical_not(from_end(owner))

    def relay(kind, k, a, first, wanted=None, chained=False):
        def visit(owner, side):
            def go():
                if first:
                    z_copy(kind, owner, a, side).wait_recv()

                @pl.when(jnp.logical_not(by_extra(kind, owner, k, a) | by_rows(k)))
                def _():
                    (start if first else wait_send)(y_copy(kind, owner, a, True))

                left = jnp.logical_not(inner & (k == 1) & from_end(owner))
                onward = exists[side] if first or a == half - 1 else exists[side] & left

                @pl.when(onward)
                def _():
                    if chained:
                        z_copy(kind, owner, a - 1, side).wait_send()
                    (start if first else wait_send)(z_copy(kind, owner, a, side))

            if wanted is not None:
                pl.when(wanted(owner))(go)
            elif kind is down_kind:
                pl.when(jnp.logical_not(by_rows(k)))(go)
            else:
                go()

        each_owner(k, visit)

    def receive_other(kind, owner, side, k):
        for a in range(half):
            extra = by_extra(kind, owner, k, a)

            @pl.when(extra)
            def _():
                extra_copy(kind, owner, a, side).wait_recv()

            @pl.when(jnp.logical_not(extra))
            def _():
                y_copy(kind, owner, a, False).wait_recv()

    inner = jnp.logical_not(at_end)
    down_first = next_inner
    up_first = (exists[0] & jnp.logical_not(next_inner[0]), exists[1] & jnp.logical_not(next_inner[1]))
    up_second = (next_inner[0] & jnp.logical_not(at_end), next_inner[1] & jnp.logical_not(at_end))
    up_third = (next_inner[0] & at_end, next_inner[1] & at_end)
    down_extra = (exists[0] & at_end, exists[1] & at_end)
    up_extra = next_inner

    own_to(down_kind, start, down_first, range(1))

    neighbour = jnp.where(me == 0, 1, last - 1)
    client = jnp.where(me == 1, 0, last)
    load_up.wait()

    @pl.when(serves)
    def _():
        for e in range(cap):
            number = fetched_ref[client, e, me]
            value = ups[me, 0, piece(0)]
            for j in range(1, stored):
                value = jnp.where(number == j, ups[me, j // half, piece(j % half)], value)
            picked[piece(e)] = value

    own_to(up_kind, start, up_first, source=picked)

    entry = jnp.broadcast_to(entry_ref[...].reshape(1, rows), (held, rows)).T
    aid[...] = jnp.zeros_like(aid)

    @pl.loop(0, groups)
    def _(o):
        number = aid[...]
        for e in range(cap):
            number = jnp.where(entry == cap * o + e, stored * o + fetched_ref[me, e, o], number)
        aid[...] = number

    lane = lax.broadcasted_iota(jnp.int32, (rows, held), 1)
    lane_adapter = lax.div(lane, rank)

    def chosen(o, h):
        return aid[...] == stored * o + half * h + lane_adapter

    load_x.wait()

    packed = row_out.shape[0]

    def row_copies():
        return (
            remote(row_out, row_in, row_sem.at[0], row_sem.at[1], {"dp": neighbour}),
            remote(code_out, code_in, row_sem.at[2], row_sem.at[3], {"dp": neighbour}),
        )

    ret_copy = remote(ret_out, ret_in, row_sem.at[4], row_sem.at[5], {"dp": client})

    def core_copy(s):
        return remote(
            part.at[2 * s], core_in.at[s], core_sem.at[0, s], core_sem.at[1, s], {"tp": other_core}
        )

    def chip_copy(s):
        far = lax.rem(chip + s + 1, chips)
        return remote(
            part.at[2 * s + 1],
            x_in.at[s],
            xs_sem.at[0, s],
            xs_sem.at[1, s],
            {"tp": CORES * far + core},
        )

    def multiply(j):
        @pl.loop(0, tiles)
        def _(n):
            load_w(j, n).wait()
            part[j, :, pl.ds(pl.multiple_of(n * tile, 128), tile)] = jnp.dot(
                x[...], w[j, n], preferred_element_type=f32
            )

    def pass_on(s):
        core_copy(s).wait_recv()
        part[2 * s + 1] = part[2 * s + 1] + core_in[s]
        chip_copy(s).start()

    @pl.loop(0, chips - 1)
    def _(s):
        multiply(2 * s)
        core_copy(s).start()

        @pl.when(s > 0)
        def _():
            pass_on(s - 1)

        multiply(2 * s + 1)

    pass_on(chips - 2)
    own_to(down_kind, start, down_first, range(1, half))

    @pl.when(inner)
    def _():
        relay(down_kind, 1, 0, True, not_from_end)

    multiply(tps - 2)
    core_copy(chips - 1).start()
    multiply(tps - 1)

    own_to(down_kind, wait_send, down_first, range(1, half))
    own_to(up_kind, start, up_third)

    @pl.when(inner)
    def _():
        relay(down_kind, 1, 0, True, from_end)

    @pl.when(at_end)
    def _():
        local = aid[...] - stored * neighbour
        uses = (local >= 0) & (local < stored)
        below = lax.broadcasted_iota(jnp.int32, (rows, rows), 1) < lax.broadcasted_iota(
            jnp.int32, (rows, rows), 0
        )
        order = jnp.dot(
            jnp.where(below, 1.0, 0.0).astype(bf16),
            jnp.where(uses, 1.0, 0.0).astype(bf16),
            preferred_element_type=f32,
        )
        spot = jnp.where(uses & (order == lane.astype(f32)), 1.0, 0.0)
        place[...] = spot.astype(bf16)
        pick = spot.T.astype(bf16)[:packed]
        row_out[...] = jnp.dot(pick, x[...], preferred_element_type=f32).astype(bf16)
        code_out[...] = jnp.dot(
            pick, local.astype(f32).astype(bf16), preferred_element_type=f32
        ).astype(bf16)
    @pl.when(at_end)
    def _():
        for a in range(half):
            relay(up_kind, 1, a, True)

    @pl.when(inner)
    def _():
        for a in range(1, half):
            relay(down_kind, 1, a, True, not_from_end)
            relay(down_kind, 1, a, True, from_end, True)

    def shrink(o, h):
        product = lax.dot_general(
            x[...], downs[o, h], (((1,), (1,)), ((), ())), preferred_element_type=f32
        )
        shr[...] += jnp.where(chosen(o, h), product, 0.0)

    shr[...] = jnp.zeros_like(shr)
    load_down.wait()

    def shrink_own(o, side):
        shrink(o, rep)

    @pl.loop(0, reps)
    def _(h):
        shrink(me, h)

    @pl.when(inner)
    def _():
        each_owner(1, shrink_own)

    relay(down_kind, 2, 0, True)
    own_to(up_kind, wait_send, up_third)

    @pl.when(at_end)
    def _():
        for c in row_copies():
            c.start()

    for a in range(1, half):
        relay(down_kind, 2, a, True)
    own_to(up_kind, start, up_second)
    each_owner(2, shrink_own)

    @pl.loop(3, groups)
    def _(k):
        for a in range(half):
            relay(down_kind, k, a, True)
            if a == half - 1:

                @pl.when(k == 3)
                def _():
                    extra_to(down_kind, start, down_extra)

        each_owner(k, shrink_own)

    def shrink_other(k, wanted):
        def visit(owner, side):
            def go():
                receive_other(down_kind, owner, side, k)
                shrink(owner, other_rep)

            pl.when(wanted(owner))(go)

        each_owner(k, visit)

    @pl.when(inner)
    def _():
        shrink_other(1, not_from_end)
        for a in range(half):
            relay(up_kind, 1, a, True, not_from_end)
        own_to(up_kind, wait_send, up_second)
        for a in range(half):
            relay(up_kind, 1, a, True, from_end, a > 0)

    @pl.when(serves)
    def _():
        for c in row_copies():
            c.wait_recv()
        code = code_in[...].astype(f32).astype(jnp.int32)
        group = lax.div(lax.broadcasted_iota(jnp.int32, (packed, held), 1), rank)
        total = jnp.zeros((packed, held), f32)
        for h in range(reps):
            product = lax.dot_general(
                row_in[...], downs[me, h], (((1,), (1,)), ((), ())), preferred_element_type=f32
            )
            total = total + jnp.where(code == half * h + group, product, 0.0)
        ret_out[...] = total
        ret_copy.start()

    @pl.when(at_end)
    def _():
        shrink_other(2, lambda owner: True)
        ret_copy.wait_recv()
        rest = ret_in[...]
        spot = place[...][:, :packed]
        for _ in range(3):
            term = rest.astype(bf16)
            rest = rest - term.astype(f32)
            shr[...] += jnp.dot(spot, term, preferred_element_type=f32)

    for a in range(half):
        relay(up_kind, 2, a, True)
    extra_to(up_kind, start, up_extra)

    @pl.when(inner)
    def _():
        shrink_other(2, lambda owner: True)
        shrink_other(1, from_end)

    @pl.loop(3, groups)
    def _(k):
        shrink_other(k, lambda owner: True)

    block = rows // half
    lane_group = lane_adapter[:block]

    def spread(value):
        total = value
        for g in range(1, half):
            total = total + pltpu.roll(value, g * rank, 1)
        return total

    whole = spread(shr[...])
    pack = jnp.zeros((block, held), f32)
    for g in range(half):
        pack = jnp.where(lane_group == g, whole[g * block : (g + 1) * block], pack)
    shr_own[...] = pack

    shr_core_copy = remote(
        shr_own, shr_core, shr_sem.at[0, chips - 1], shr_sem.at[1, chips - 1], {"tp": other_core}
    )

    def shr_copy(s):
        far = lax.rem(chip + s + 1, chips)
        return remote(
            shr_pair,
            shr_in.at[s],
            shr_sem.at[0, s],
            shr_sem.at[1, s],
            {"tp": CORES * far + core},
        )

    shr_core_copy.start()
    base = part.at[tps - 1]
    core_copy(chips - 1).wait_recv()
    base[...] += core_in[chips - 1]
    shr_core_copy.wait_recv()
    shr_pair[...] = shr_own[...] + shr_core[...]

    @pl.loop(0, chips - 1)
    def _(s):
        shr_copy(s).start()

    @pl.loop(0, chips - 1)
    def _(s):
        chip_copy(s).wait_recv()
        base[...] += x_in[s]

    @pl.loop(3, groups)
    def _(k):
        for a in range(half):
            relay(up_kind, k, a, True)

    shr_own_sum = shr_pair[...]
    for s in range(chips - 1):
        shr_copy(s).wait_recv()
        shr_own_sum = shr_own_sum + shr_in[s]
    for g in range(half):
        shr[g * block : (g + 1) * block] = spread(jnp.where(lane_group == g, shr_own_sum, 0.0))

    def expand(o):
        masks = [chosen(o, h) for h in range(reps)]
        expand_by(masks, ups[o].reshape(reps * held, width))

    def expand_by(masks, up):
        factor = jnp.concatenate(
            [jnp.where(mask, adapter_scale * shr[...], 0.0) for mask in masks], axis=1
        )
        high = factor.astype(bf16)
        low = (factor - high.astype(f32)).astype(bf16)
        base[...] += jnp.dot(high, up, preferred_element_type=f32) + jnp.dot(
            low, up, preferred_element_type=f32
        )

    expand(me)

    @pl.when(at_end)
    def _():
        number = jnp.zeros((rows, held), jnp.int32)
        for e in range(cap):
            number = jnp.where(lane_adapter == e, fetched_ref[me, e, neighbour], number)
        expand_by([aid[...] == stored * neighbour + number], ups[neighbour, rep])

    @pl.when(inner)
    def _():
        def visit(owner, side):
            receive_other(up_kind, owner, side, 1)
            expand(owner)

        each_owner(1, visit)

    @pl.loop(2, groups)
    def _(k):
        def visit(owner, side):
            receive_other(up_kind, owner, side, k)
            expand(owner)

        each_owner(k, visit)

    out_ref[...] = base[...].astype(out_ref.dtype)

    @pl.loop(0, chips)
    def _(s):
        core_copy(s).wait_send()

    @pl.loop(0, chips - 1)
    def _(s):
        chip_copy(s).wait_send()

    @pl.when(at_end)
    def _():
        for c in row_copies():
            c.wait_send()

    @pl.when(serves)
    def _():
        ret_copy.wait_send()

    own_to(down_kind, wait_send, down_first, range(1))
    extra_to(down_kind, wait_send, down_extra)
    own_to(up_kind, wait_send, up_first, source=picked)
    shr_core_copy.wait_send()

    @pl.loop(0, chips - 1)
    def _(s):
        shr_copy(s).wait_send()

    extra_to(up_kind, wait_send, up_extra)

    @pl.loop(1, groups)
    def _(k):
        for kind in (down_kind, up_kind):
            for a in range(half):
                relay(kind, k, a, False)


def body(
    sizes,
    attention_input,
    output_weight,
    adapter_down_weight,
    adapter_up_weight,
    fetched_local_numbers,
    request_adapter_entry,
):
    reps, groups, tps = sizes
    chips = tps // CORES
    rows, features = attention_input.shape
    stored, _, rank = adapter_down_weight.shape
    width = adapter_up_weight.shape[2]
    half = stored // reps
    held = half * rank
    tile = min(512, width)
    tiles = width // tile
    down = adapter_down_weight.transpose(0, 2, 1).reshape(reps, held, features)
    up = adapter_up_weight.reshape(reps, held, width)
    cap = fetched_local_numbers.shape[2]
    packed = rows * cap // groups
    any_space = pl.BlockSpec(memory_space=pl.ANY)
    vmem = pl.BlockSpec(memory_space=pltpu.VMEM)
    dma = pltpu.SemaphoreType.DMA
    f32, bf16 = jnp.float32, jnp.bfloat16
    return pl.pallas_call(
        functools.partial(kernel, (reps, groups, tps, rank)),
        out_shape=pltpu.VMEM((rows, width), bf16),
        in_specs=[vmem, pl.BlockSpec(memory_space=pltpu.SMEM)] + [any_space] * 4,
        out_specs=vmem,
        scratch_shapes=[
            pltpu.VMEM((rows, features), bf16),
            pltpu.VMEM((tps, tiles, features, tile), bf16),
            pltpu.VMEM((groups, reps, held, features), bf16),
            pltpu.VMEM((groups, reps, held, width), bf16),
            pltpu.VMEM((tps, rows, width), f32),
            pltpu.VMEM((chips, rows, width), f32),
            pltpu.VMEM((chips - 1, rows, width), f32),
            pltpu.VMEM((rows, held), f32),
            pltpu.VMEM((rows // half, held), f32),
            pltpu.VMEM((rows // half, held), f32),
            pltpu.VMEM((rows // half, held), f32),
            pltpu.VMEM((chips - 1, rows // half, held), f32),
            pltpu.VMEM((held, width), bf16),
            pltpu.VMEM((rows, held), jnp.int32),
            pltpu.VMEM((rows, held), bf16),
            pltpu.VMEM((packed, features), bf16),
            pltpu.VMEM((packed, features), bf16),
            pltpu.VMEM((packed, held), bf16),
            pltpu.VMEM((packed, held), bf16),
            pltpu.VMEM((packed, held), f32),
            pltpu.VMEM((packed, held), f32),
            dma((3,)),
            dma((tps, tiles)),
            dma((2, chips)),
            dma((2, chips - 1)),
            dma((2, chips)),
            dma((3, groups, half)),
            dma((2, groups, half)),
            dma((4, half)),
            dma((3, groups, half)),
            dma((2, groups, half)),
            dma((4, half)),
            dma((6,)),
        ],
        compiler_params=pltpu.CompilerParams(
            collective_id=0, has_side_effects=True, vmem_limit_bytes=56 * 1024 * 1024
        ),
    )(
        request_adapter_entry,
        fetched_local_numbers.transpose(0, 2, 1),
        attention_input,
        output_weight,
        down,
        up,
    )


def solution(mesh):
    in_specs = (
        P(("rep", "dp"), "tp"),
        P("tp", None),
        P("dp", "tp", None),
        P("dp", None, "tp"),
        P("rep", None, None),
        P(("rep", "dp")),
    )
    out_specs = P(("rep", "dp"), "tp")
    sizes = (mesh.shape["rep"], mesh.shape["dp"], mesh.shape["tp"])
    return jax.shard_map(
        functools.partial(body, sizes),
        mesh=mesh,
        in_specs=in_specs,
        out_specs=out_specs,
        check_vma=False,
    )
```

```python
import functools

import jax
import jax.numpy as jnp
from jax import lax
from jax.experimental import pallas as pl
from jax.experimental.pallas import tpu as pltpu
from jax.sharding import PartitionSpec as P

adapter_scale = 0.5
CORES = 2


def kernel(
    sizes,
    entry_ref,
    fetched_ref,
    x_hbm,
    w_hbm,
    down_hbm,
    up_hbm,
    out_ref,
    x,
    w,
    downs,
    ups,
    part,
    core_in,
    x_in,
    shr,
    shr_own,
    shr_core,
    shr_pair,
    shr_in,
    picked,
    aid,
    place,
    row_out,
    row_in,
    code_out,
    code_in,
    ret_out,
    ret_in,
    local_sem,
    w_sem,
    core_sem,
    xs_sem,
    shr_sem,
    zd_sem,
    yd_sem,
    ed_sem,
    zu_sem,
    yu_sem,
    eu_sem,
    row_sem,
):
    reps, groups, tps, rank = sizes
    chips = tps // CORES
    rep = lax.axis_index("rep")
    me = lax.axis_index("dp")
    tp = lax.axis_index("tp")
    core = lax.rem(tp, CORES)
    chip = lax.div(tp, CORES)
    other_core = CORES * chip + (1 - core)
    other_rep = 1 - rep
    rows = x.shape[0]
    width = out_ref.shape[1]
    held = downs.shape[2]
    half = held // rank
    stored = half * reps
    cap = fetched_ref.shape[1]
    tiles, tile = w.shape[1], w.shape[3]
    last = groups - 1
    f32, bf16 = jnp.float32, jnp.bfloat16

    def remote(src, dst, send, recv, target):
        return pltpu.make_async_remote_copy(
            src_ref=src,
            dst_ref=dst,
            send_sem=send,
            recv_sem=recv,
            device_id=target,
            device_id_type=pl.DeviceIdType.MESH,
        )

    def start(c):
        c.start()

    def wait_send(c):
        c.wait_send()

    load_x = pltpu.make_async_copy(x_hbm, x, local_sem.at[0])
    load_down = pltpu.make_async_copy(down_hbm, downs.at[me], local_sem.at[1])
    load_up = pltpu.make_async_copy(up_hbm, ups.at[me], local_sem.at[2])
    load_x.start()
    load_up.start()

    def column_of(j):
        far = lax.rem(chip + lax.div(j, 2) + 1, chips)
        return CORES * far + jnp.where(lax.rem(j, 2) == 0, 1 - core, core)

    def load_w(j, n):
        first = pl.multiple_of(column_of(j) * width + n * tile, 128)
        return pltpu.make_async_copy(
            w_hbm.at[:, pl.ds(first, tile)], w.at[j, n], w_sem.at[j, n]
        )

    @pl.loop(0, tps)
    def _(j):
        for n in range(tiles):
            load_w(j, n).start()

    load_down.start()

    barrier = pltpu.get_barrier_semaphore()

    def greet(target):
        pl.semaphore_signal(
            barrier, inc=1, device_id=target, device_id_type=pl.DeviceIdType.MESH
        )

    @pl.when(me > 0)
    def _():
        greet({"dp": me - 1})

    @pl.when(me < last)
    def _():
        greet({"dp": me + 1})

    greet({"rep": other_rep})

    @pl.loop(1, tps)
    def _(q):
        greet({"tp": lax.rem(tp + q, tps)})

    edges = jnp.where(me > 0, 1, 0) + jnp.where(me < last, 1, 0)
    pl.semaphore_wait(barrier, tps + edges)

    down_kind = (downs, down_hbm, zd_sem, yd_sem, ed_sem)
    up_kind = (ups, up_hbm, zu_sem, yu_sem, eu_sem)
    at_end = (me == 0) | (me == last)
    serves = (me == 1) | (me == last - 1)
    step = (-1, 1)
    exists = (me > 0, me < last)
    next_inner = (me > 1, me < last - 1)

    def piece(a):
        return pl.ds(a * rank, rank)

    def z_copy(kind, owner, a, side, source=None):
        buffer, _, z = kind[:3]
        src = buffer.at[owner, rep, piece(a)] if source is None else source.at[piece(a)]
        return remote(
            src,
            buffer.at[owner, rep, piece(a)],
            z.at[side, owner, a],
            z.at[2, owner, a],
            {"dp": me + step[side]},
        )

    def extra_copy(kind, owner, a, side):
        buffer, source, extra = kind[0], kind[1], kind[4]
        return remote(
            source.at[other_rep, piece(a)],
            buffer.at[owner, other_rep, piece(a)],
            extra.at[side, a],
            extra.at[3 - side, a],
            {"dp": me + step[side]},
        )

    def y_copy(kind, owner, a, mine):
        buffer, y = kind[0], kind[3]
        where = buffer.at[owner, rep if mine else other_rep, piece(a)]
        return remote(where, where, y.at[0, owner, a], y.at[1, owner, a], {"rep": other_rep})

    def own_to(kind, act, sides, pieces=range(half), source=None):
        for side in (0, 1):

            @pl.when(sides[side])
            def _():
                for a in pieces:
                    act(z_copy(kind, me, a, side, kind[1].at[rep] if source is None else source))

    def extra_to(kind, act, sides):
        for side in (0, 1):

            @pl.when(sides[side])
            def _():
                for a in extra_pieces(kind):
                    act(extra_copy(kind, me, a, side))

    def each_owner(k, visit):
        for side in (0, 1):
            owner = me - step[side] * k

            @pl.when((owner >= 0) & (owner < groups))
            def _():
                visit(owner, side)

    def by_rows(k):
        return at_end & (k == 1)

    def extra_pieces(kind):
        return range(max(half // 2, 1)) if kind is down_kind else range(half)

    def by_extra(kind, owner, k, a):
        if a not in extra_pieces(kind):
            return False
        if kind is down_kind:
            return (k == 1) & ((owner == 0) | (owner == last))
        return (k == 1) & (me > 0) & (me < last)

    def from_end(owner):
        return (owner == 0) | (owner == last)

    def not_from_end(owner):
        return jnp.logical_not(from_end(owner))

    def relay(kind, k, a, first, wanted=None, chained=False):
        def visit(owner, side):
            def go():
                if first:
                    z_copy(kind, owner, a, side).wait_recv()

                @pl.when(jnp.logical_not(by_extra(kind, owner, k, a) | by_rows(k)))
                def _():
                    (start if first else wait_send)(y_copy(kind, owner, a, True))

                left = jnp.logical_not(inner & (k == 1) & from_end(owner))
                onward = exists[side] if first or a == half - 1 else exists[side] & left

                @pl.when(onward)
                def _():
                    if chained:
                        z_copy(kind, owner, a - 1, side).wait_send()
                    (start if first else wait_send)(z_copy(kind, owner, a, side))

            if wanted is not None:
                pl.when(wanted(owner))(go)
            elif kind is down_kind:
                pl.when(jnp.logical_not(by_rows(k)))(go)
            else:
                go()

        each_owner(k, visit)

    def receive_other(kind, owner, side, k):
        for a in range(half):
            extra = by_extra(kind, owner, k, a)

            @pl.when(extra)
            def _():
                extra_copy(kind, owner, a, side).wait_recv()

            @pl.when(jnp.logical_not(extra))
            def _():
                y_copy(kind, owner, a, False).wait_recv()

    inner = jnp.logical_not(at_end)
    down_first = next_inner
    up_first = (exists[0] & jnp.logical_not(next_inner[0]), exists[1] & jnp.logical_not(next_inner[1]))
    up_second = (next_inner[0] & jnp.logical_not(at_end), next_inner[1] & jnp.logical_not(at_end))
    up_third = (next_inner[0] & at_end, next_inner[1] & at_end)
    down_extra = (exists[0] & at_end, exists[1] & at_end)
    up_extra = next_inner

    own_to(down_kind, start, down_first, range(1))

    neighbour = jnp.where(me == 0, 1, last - 1)
    client = jnp.where(me == 1, 0, last)
    load_up.wait()

    @pl.when(serves)
    def _():
        for e in range(cap):
            number = fetched_ref[client, e, me]
            value = ups[me, 0, piece(0)]
            for j in range(1, stored):
                value = jnp.where(number == j, ups[me, j // half, piece(j % half)], value)
            picked[piece(e)] = value

    own_to(up_kind, start, up_first, source=picked)

    entry = jnp.broadcast_to(entry_ref[...].reshape(1, rows), (held, rows)).T
    aid[...] = jnp.zeros_like(aid)

    @pl.loop(0, groups)
    def _(o):
        number = aid[...]
        for e in range(cap):
            number = jnp.where(entry == cap * o + e, stored * o + fetched_ref[me, e, o], number)
        aid[...] = number

    lane = lax.broadcasted_iota(jnp.int32, (rows, held), 1)
    lane_adapter = lax.div(lane, rank)

    def chosen(o, h):
        return aid[...] == stored * o + half * h + lane_adapter

    load_x.wait()

    packed = row_out.shape[0]

    def row_copies():
        return (
            remote(row_out, row_in, row_sem.at[0], row_sem.at[1], {"dp": neighbour}),
            remote(code_out, code_in, row_sem.at[2], row_sem.at[3], {"dp": neighbour}),
        )

    ret_copy = remote(ret_out, ret_in, row_sem.at[4], row_sem.at[5], {"dp": client})

    def core_copy(s):
        return remote(
            part.at[2 * s], core_in.at[s], core_sem.at[0, s], core_sem.at[1, s], {"tp": other_core}
        )

    def chip_copy(s):
        far = lax.rem(chip + s + 1, chips)
        return remote(
            part.at[2 * s + 1],
            x_in.at[s],
            xs_sem.at[0, s],
            xs_sem.at[1, s],
            {"tp": CORES * far + core},
        )

    def multiply(j):
        @pl.loop(0, tiles)
        def _(n):
            load_w(j, n).wait()
            part[j, :, pl.ds(pl.multiple_of(n * tile, 128), tile)] = jnp.dot(
                x[...], w[j, n], preferred_element_type=f32
            )

    def pass_on(s):
        core_copy(s).wait_recv()
        part[2 * s + 1] = part[2 * s + 1] + core_in[s]
        chip_copy(s).start()

    @pl.loop(0, chips - 1)
    def _(s):
        multiply(2 * s)
        core_copy(s).start()

        @pl.when(s > 0)
        def _():
            pass_on(s - 1)

        multiply(2 * s + 1)

    pass_on(chips - 2)
    own_to(down_kind, start, down_first, range(1, half))

    @pl.when(inner)
    def _():
        relay(down_kind, 1, 0, True, not_from_end)

    multiply(tps - 2)
    core_copy(chips - 1).start()
    multiply(tps - 1)

    own_to(down_kind, wait_send, down_first, range(1, half))
    own_to(up_kind, start, up_third)

    @pl.when(inner)
    def _():
        relay(down_kind, 1, 0, True, from_end)

    @pl.when(at_end)
    def _():
        local = aid[...] - stored * neighbour
        uses = (local >= 0) & (local < stored)
        below = lax.broadcasted_iota(jnp.int32, (rows, rows), 1) < lax.broadcasted_iota(
            jnp.int32, (rows, rows), 0
        )
        order = jnp.dot(
            jnp.where(below, 1.0, 0.0).astype(bf16),
            jnp.where(uses, 1.0, 0.0).astype(bf16),
            preferred_element_type=f32,
        )
        spot = jnp.where(uses & (order == lane.astype(f32)), 1.0, 0.0)
        place[...] = spot.astype(bf16)
        pick = spot.T.astype(bf16)[:packed]
        row_out[...] = jnp.dot(pick, x[...], preferred_element_type=f32).astype(bf16)
        code_out[...] = jnp.dot(
            pick, local.astype(f32).astype(bf16), preferred_element_type=f32
        ).astype(bf16)
    @pl.when(at_end)
    def _():
        for a in range(half):
            relay(up_kind, 1, a, True)

    @pl.when(inner)
    def _():
        for a in range(1, half):
            relay(down_kind, 1, a, True, not_from_end)
            relay(down_kind, 1, a, True, from_end, True)

    def shrink(o, h):
        product = lax.dot_general(
            x[...], downs[o, h], (((1,), (1,)), ((), ())), preferred_element_type=f32
        )
        shr[...] += jnp.where(chosen(o, h), product, 0.0)

    shr[...] = jnp.zeros_like(shr)
    load_down.wait()

    def shrink_own(o, side):
        shrink(o, rep)

    @pl.loop(0, reps)
    def _(h):
        shrink(me, h)

    @pl.when(inner)
    def _():
        each_owner(1, shrink_own)

    relay(down_kind, 2, 0, True)
    own_to(up_kind, wait_send, up_third)

    @pl.when(at_end)
    def _():
        for c in row_copies():
            c.start()

    for a in range(1, half):
        relay(down_kind, 2, a, True)
    own_to(up_kind, start, up_second)
    each_owner(2, shrink_own)

    @pl.loop(3, groups)
    def _(k):
        for a in range(half):
            relay(down_kind, k, a, True)
            if a == half - 1:

                @pl.when(k == 3)
                def _():
                    extra_to(down_kind, start, down_extra)

        each_owner(k, shrink_own)

    def shrink_other(k, wanted):
        def visit(owner, side):
            def go():
                receive_other(down_kind, owner, side, k)
                shrink(owner, other_rep)

            pl.when(wanted(owner))(go)

        each_owner(k, visit)

    @pl.when(serves)
    def _():
        for c in row_copies():
            c.wait_recv()
        code = code_in[...].astype(f32).astype(jnp.int32)
        group = lax.div(lax.broadcasted_iota(jnp.int32, (packed, held), 1), rank)
        total = jnp.zeros((packed, held), f32)
        for h in range(reps):
            product = lax.dot_general(
                row_in[...], downs[me, h], (((1,), (1,)), ((), ())), preferred_element_type=f32
            )
            total = total + jnp.where(code == half * h + group, product, 0.0)
        ret_out[...] = total
        ret_copy.start()

    @pl.when(inner)
    def _():
        shrink_other(1, not_from_end)
        for a in range(half):
            relay(up_kind, 1, a, True, not_from_end)
        own_to(up_kind, wait_send, up_second)
        for a in range(half):
            relay(up_kind, 1, a, True, from_end, a > 0)

    @pl.when(at_end)
    def _():
        shrink_other(2, lambda owner: True)
        ret_copy.wait_recv()
        rest = ret_in[...]
        spot = place[...][:, :packed]
        for _ in range(3):
            term = rest.astype(bf16)
            rest = rest - term.astype(f32)
            shr[...] += jnp.dot(spot, term, preferred_element_type=f32)

    for a in range(half):
        relay(up_kind, 2, a, True)
    extra_to(up_kind, start, up_extra)

    @pl.when(inner)
    def _():
        shrink_other(2, lambda owner: True)
        shrink_other(1, from_end)

    @pl.loop(3, groups)
    def _(k):
        shrink_other(k, lambda owner: True)

    block = rows // half
    lane_group = lane_adapter[:block]

    def spread(value):
        total = value
        for g in range(1, half):
            total = total + pltpu.roll(value, g * rank, 1)
        return total

    whole = spread(shr[...])
    pack = jnp.zeros((block, held), f32)
    for g in range(half):
        pack = jnp.where(lane_group == g, whole[g * block : (g + 1) * block], pack)
    shr_own[...] = pack

    shr_core_copy = remote(
        shr_own, shr_core, shr_sem.at[0, chips - 1], shr_sem.at[1, chips - 1], {"tp": other_core}
    )

    def shr_copy(s):
        far = lax.rem(chip + s + 1, chips)
        return remote(
            shr_pair,
            shr_in.at[s],
            shr_sem.at[0, s],
            shr_sem.at[1, s],
            {"tp": CORES * far + core},
        )

    shr_core_copy.start()
    base = part.at[tps - 1]
    core_copy(chips - 1).wait_recv()
    base[...] += core_in[chips - 1]
    shr_core_copy.wait_recv()
    shr_pair[...] = shr_own[...] + shr_core[...]

    @pl.loop(0, chips - 1)
    def _(s):
        shr_copy(s).start()

    @pl.loop(0, chips - 1)
    def _(s):
        chip_copy(s).wait_recv()
        base[...] += x_in[s]

    @pl.loop(3, groups)
    def _(k):
        for a in range(half):
            relay(up_kind, k, a, True)

    shr_own_sum = shr_pair[...]
    for s in range(chips - 1):
        shr_copy(s).wait_recv()
        shr_own_sum = shr_own_sum + shr_in[s]
    for g in range(half):
        shr[g * block : (g + 1) * block] = spread(jnp.where(lane_group == g, shr_own_sum, 0.0))

    def expand(o):
        masks = [chosen(o, h) for h in range(reps)]
        expand_by(masks, ups[o].reshape(reps * held, width))

    def expand_by(masks, up):
        factor = jnp.concatenate(
            [jnp.where(mask, adapter_scale * shr[...], 0.0) for mask in masks], axis=1
        )
        high = factor.astype(bf16)
        low = (factor - high.astype(f32)).astype(bf16)
        base[...] += jnp.dot(high, up, preferred_element_type=f32) + jnp.dot(
            low, up, preferred_element_type=f32
        )

    expand(me)

    @pl.when(at_end)
    def _():
        number = jnp.zeros((rows, held), jnp.int32)
        for e in range(cap):
            number = jnp.where(lane_adapter == e, fetched_ref[me, e, neighbour], number)
        expand_by([aid[...] == stored * neighbour + number], ups[neighbour, rep])

    @pl.when(inner)
    def _():
        def visit(owner, side):
            receive_other(up_kind, owner, side, 1)
            expand(owner)

        each_owner(1, visit)

    @pl.loop(2, groups)
    def _(k):
        def visit(owner, side):
            receive_other(up_kind, owner, side, k)
            expand(owner)

        each_owner(k, visit)

    out_ref[...] = base[...].astype(out_ref.dtype)

    @pl.loop(0, chips)
    def _(s):
        core_copy(s).wait_send()

    @pl.loop(0, chips - 1)
    def _(s):
        chip_copy(s).wait_send()

    @pl.when(at_end)
    def _():
        for c in row_copies():
            c.wait_send()

    @pl.when(serves)
    def _():
        ret_copy.wait_send()

    own_to(down_kind, wait_send, down_first, range(1))
    extra_to(down_kind, wait_send, down_extra)
    own_to(up_kind, wait_send, up_first, source=picked)
    shr_core_copy.wait_send()

    @pl.loop(0, chips - 1)
    def _(s):
        shr_copy(s).wait_send()

    extra_to(up_kind, wait_send, up_extra)

    @pl.loop(1, groups)
    def _(k):
        for kind in (down_kind, up_kind):
            for a in range(half):
                relay(kind, k, a, False)


def body(
    sizes,
    attention_input,
    output_weight,
    adapter_down_weight,
    adapter_up_weight,
    fetched_local_numbers,
    request_adapter_entry,
):
    reps, groups, tps = sizes
    chips = tps // CORES
    rows, features = attention_input.shape
    stored, _, rank = adapter_down_weight.shape
    width = adapter_up_weight.shape[2]
    half = stored // reps
    held = half * rank
    tile = min(512, width)
    tiles = width // tile
    down = adapter_down_weight.transpose(0, 2, 1).reshape(reps, held, features)
    up = adapter_up_weight.reshape(reps, held, width)
    cap = fetched_local_numbers.shape[2]
    packed = rows * cap // groups
    any_space = pl.BlockSpec(memory_space=pl.ANY)
    vmem = pl.BlockSpec(memory_space=pltpu.VMEM)
    dma = pltpu.SemaphoreType.DMA
    f32, bf16 = jnp.float32, jnp.bfloat16
    return pl.pallas_call(
        functools.partial(kernel, (reps, groups, tps, rank)),
        out_shape=pltpu.VMEM((rows, width), bf16),
        in_specs=[vmem, pl.BlockSpec(memory_space=pltpu.SMEM)] + [any_space] * 4,
        out_specs=vmem,
        scratch_shapes=[
            pltpu.VMEM((rows, features), bf16),
            pltpu.VMEM((tps, tiles, features, tile), bf16),
            pltpu.VMEM((groups, reps, held, features), bf16),
            pltpu.VMEM((groups, reps, held, width), bf16),
            pltpu.VMEM((tps, rows, width), f32),
            pltpu.VMEM((chips, rows, width), f32),
            pltpu.VMEM((chips - 1, rows, width), f32),
            pltpu.VMEM((rows, held), f32),
            pltpu.VMEM((rows // half, held), f32),
            pltpu.VMEM((rows // half, held), f32),
            pltpu.VMEM((rows // half, held), f32),
            pltpu.VMEM((chips - 1, rows // half, held), f32),
            pltpu.VMEM((held, width), bf16),
            pltpu.VMEM((rows, held), jnp.int32),
            pltpu.VMEM((rows, held), bf16),
            pltpu.VMEM((packed, features), bf16),
            pltpu.VMEM((packed, features), bf16),
            pltpu.VMEM((packed, held), bf16),
            pltpu.VMEM((packed, held), bf16),
            pltpu.VMEM((packed, held), f32),
            pltpu.VMEM((packed, held), f32),
            dma((3,)),
            dma((tps, tiles)),
            dma((2, chips)),
            dma((2, chips - 1)),
            dma((2, chips)),
            dma((3, groups, half)),
            dma((2, groups, half)),
            dma((4, half)),
            dma((3, groups, half)),
            dma((2, groups, half)),
            dma((4, half)),
            dma((6,)),
        ],
        compiler_params=pltpu.CompilerParams(
            collective_id=0, has_side_effects=True, vmem_limit_bytes=56 * 1024 * 1024
        ),
    )(
        request_adapter_entry,
        fetched_local_numbers.transpose(0, 2, 1),
        attention_input,
        output_weight,
        down,
        up,
    )


def solution(mesh):
    in_specs = (
        P(("rep", "dp"), "tp"),
        P("tp", None),
        P("dp", "tp", None),
        P("dp", None, "tp"),
        P("rep", None, None),
        P(("rep", "dp")),
    )
    out_specs = P(("rep", "dp"), "tp")
    sizes = (mesh.shape["rep"], mesh.shape["dp"], mesh.shape["tp"])
    return jax.shard_map(
        functools.partial(body, sizes),
        mesh=mesh,
        in_specs=in_specs,
        out_specs=out_specs,
        check_vma=False,
    )
```

```python
import functools

import jax
import jax.numpy as jnp
from jax import lax
from jax.experimental import pallas as pl
from jax.experimental.pallas import tpu as pltpu
from jax.sharding import PartitionSpec as P

adapter_scale = 0.5
CORES = 2


def kernel(
    sizes,
    entry_ref,
    fetched_ref,
    x_hbm,
    w_hbm,
    down_hbm,
    up_hbm,
    out_ref,
    x,
    w,
    downs,
    ups,
    part,
    core_in,
    x_in,
    shr,
    shr_own,
    shr_core,
    shr_pair,
    shr_in,
    picked,
    aid,
    place,
    row_out,
    row_in,
    code_out,
    code_in,
    ret_out,
    ret_in,
    local_sem,
    w_sem,
    core_sem,
    xs_sem,
    shr_sem,
    zd_sem,
    yd_sem,
    ed_sem,
    zu_sem,
    yu_sem,
    eu_sem,
    row_sem,
):
    reps, groups, tps, rank = sizes
    chips = tps // CORES
    rep = lax.axis_index("rep")
    me = lax.axis_index("dp")
    tp = lax.axis_index("tp")
    core = lax.rem(tp, CORES)
    chip = lax.div(tp, CORES)
    other_core = CORES * chip + (1 - core)
    other_rep = 1 - rep
    rows = x.shape[0]
    width = out_ref.shape[1]
    held = downs.shape[2]
    half = held // rank
    stored = half * reps
    cap = fetched_ref.shape[1]
    tiles, tile = w.shape[1], w.shape[3]
    last = groups - 1
    f32, bf16 = jnp.float32, jnp.bfloat16

    def remote(src, dst, send, recv, target):
        return pltpu.make_async_remote_copy(
            src_ref=src,
            dst_ref=dst,
            send_sem=send,
            recv_sem=recv,
            device_id=target,
            device_id_type=pl.DeviceIdType.MESH,
        )

    def start(c):
        c.start()

    def wait_send(c):
        c.wait_send()

    load_x = pltpu.make_async_copy(x_hbm, x, local_sem.at[0])
    load_down = pltpu.make_async_copy(down_hbm, downs.at[me], local_sem.at[1])
    load_up = pltpu.make_async_copy(up_hbm, ups.at[me], local_sem.at[2])
    load_x.start()
    load_up.start()

    def column_of(j):
        far = lax.rem(chip + lax.div(j, 2) + 1, chips)
        return CORES * far + jnp.where(lax.rem(j, 2) == 0, 1 - core, core)

    def load_w(j, n):
        first = pl.multiple_of(column_of(j) * width + n * tile, 128)
        return pltpu.make_async_copy(
            w_hbm.at[:, pl.ds(first, tile)], w.at[j, n], w_sem.at[j, n]
        )

    @pl.loop(0, tps)
    def _(j):
        for n in range(tiles):
            load_w(j, n).start()

    load_down.start()

    barrier = pltpu.get_barrier_semaphore()

    def greet(target):
        pl.semaphore_signal(
            barrier, inc=1, device_id=target, device_id_type=pl.DeviceIdType.MESH
        )

    @pl.when(me > 0)
    def _():
        greet({"dp": me - 1})

    @pl.when(me < last)
    def _():
        greet({"dp": me + 1})

    greet({"rep": other_rep})

    @pl.loop(1, tps)
    def _(q):
        greet({"tp": lax.rem(tp + q, tps)})

    edges = jnp.where(me > 0, 1, 0) + jnp.where(me < last, 1, 0)
    pl.semaphore_wait(barrier, tps + edges)

    down_kind = (downs, down_hbm, zd_sem, yd_sem, ed_sem)
    up_kind = (ups, up_hbm, zu_sem, yu_sem, eu_sem)
    at_end = (me == 0) | (me == last)
    serves = (me == 1) | (me == last - 1)
    step = (-1, 1)
    exists = (me > 0, me < last)
    next_inner = (me > 1, me < last - 1)

    def piece(a):
        return pl.ds(a * rank, rank)

    def z_copy(kind, owner, a, side, source=None):
        buffer, _, z = kind[:3]
        src = buffer.at[owner, rep, piece(a)] if source is None else source.at[piece(a)]
        return remote(
            src,
            buffer.at[owner, rep, piece(a)],
            z.at[side, owner, a],
            z.at[2, owner, a],
            {"dp": me + step[side]},
        )

    def extra_copy(kind, owner, a, side):
        buffer, source, extra = kind[0], kind[1], kind[4]
        return remote(
            source.at[other_rep, piece(a)],
            buffer.at[owner, other_rep, piece(a)],
            extra.at[side, a],
            extra.at[3 - side, a],
            {"dp": me + step[side]},
        )

    def y_copy(kind, owner, a, mine):
        buffer, y = kind[0], kind[3]
        where = buffer.at[owner, rep if mine else other_rep, piece(a)]
        return remote(where, where, y.at[0, owner, a], y.at[1, owner, a], {"rep": other_rep})

    def own_to(kind, act, sides, pieces=range(half), source=None):
        for side in (0, 1):

            @pl.when(sides[side])
            def _():
                for a in pieces:
                    act(z_copy(kind, me, a, side, kind[1].at[rep] if source is None else source))

    def extra_to(kind, act, sides):
        for side in (0, 1):

            @pl.when(sides[side])
            def _():
                for a in extra_pieces(kind):
                    act(extra_copy(kind, me, a, side))

    def each_owner(k, visit):
        for side in (0, 1):
            owner = me - step[side] * k

            @pl.when((owner >= 0) & (owner < groups))
            def _():
                visit(owner, side)

    def by_rows(k):
        return at_end & (k == 1)

    def extra_pieces(kind):
        return range(max(half // 2, 1)) if kind is down_kind else range(half)

    def by_extra(kind, owner, k, a):
        if a not in extra_pieces(kind):
            return False
        if kind is down_kind:
            return (k == 1) & ((owner == 0) | (owner == last))
        return (k == 1) & (me > 0) & (me < last)

    def from_end(owner):
        return (owner == 0) | (owner == last)

    def not_from_end(owner):
        return jnp.logical_not(from_end(owner))

    def relay(kind, k, a, first, wanted=None, chained=False):
        def visit(owner, side):
            def go():
                if first:
                    z_copy(kind, owner, a, side).wait_recv()

                @pl.when(jnp.logical_not(by_extra(kind, owner, k, a) | by_rows(k)))
                def _():
                    (start if first else wait_send)(y_copy(kind, owner, a, True))

                left = jnp.logical_not(inner & (k == 1) & from_end(owner))
                onward = exists[side] if first or a == half - 1 else exists[side] & left

                @pl.when(onward)
                def _():
                    if chained:
                        z_copy(kind, owner, a - 1, side).wait_send()
                    (start if first else wait_send)(z_copy(kind, owner, a, side))

            if wanted is not None:
                pl.when(wanted(owner))(go)
            elif kind is down_kind:
                pl.when(jnp.logical_not(by_rows(k)))(go)
            else:
                go()

        each_owner(k, visit)

    def receive_other(kind, owner, side, k):
        for a in range(half):
            extra = by_extra(kind, owner, k, a)

            @pl.when(extra)
            def _():
                extra_copy(kind, owner, a, side).wait_recv()

            @pl.when(jnp.logical_not(extra))
            def _():
                y_copy(kind, owner, a, False).wait_recv()

    inner = jnp.logical_not(at_end)
    down_first = next_inner
    up_first = (exists[0] & jnp.logical_not(next_inner[0]), exists[1] & jnp.logical_not(next_inner[1]))
    up_second = (next_inner[0] & jnp.logical_not(at_end), next_inner[1] & jnp.logical_not(at_end))
    up_third = (next_inner[0] & at_end, next_inner[1] & at_end)
    down_extra = (exists[0] & at_end, exists[1] & at_end)
    up_extra = next_inner

    own_to(down_kind, start, down_first, range(1))

    neighbour = jnp.where(me == 0, 1, last - 1)
    client = jnp.where(me == 1, 0, last)
    load_up.wait()

    @pl.when(serves)
    def _():
        for e in range(cap):
            number = fetched_ref[client, e, me]
            value = ups[me, 0, piece(0)]
            for j in range(1, stored):
                value = jnp.where(number == j, ups[me, j // half, piece(j % half)], value)
            picked[piece(e)] = value

    own_to(up_kind, start, up_first, source=picked)

    entry = jnp.broadcast_to(entry_ref[...].reshape(1, rows), (held, rows)).T
    aid[...] = jnp.zeros_like(aid)

    @pl.loop(0, groups)
    def _(o):
        number = aid[...]
        for e in range(cap):
            number = jnp.where(entry == cap * o + e, stored * o + fetched_ref[me, e, o], number)
        aid[...] = number

    lane = lax.broadcasted_iota(jnp.int32, (rows, held), 1)
    lane_adapter = lax.div(lane, rank)

    def chosen(o, h):
        return aid[...] == stored * o + half * h + lane_adapter

    load_x.wait()

    packed = row_out.shape[0]

    def row_copies():
        return (
            remote(row_out, row_in, row_sem.at[0], row_sem.at[1], {"dp": neighbour}),
            remote(code_out, code_in, row_sem.at[2], row_sem.at[3], {"dp": neighbour}),
        )

    ret_copy = remote(ret_out, ret_in, row_sem.at[4], row_sem.at[5], {"dp": client})

    def core_copy(s):
        return remote(
            part.at[2 * s], core_in.at[s], core_sem.at[0, s], core_sem.at[1, s], {"tp": other_core}
        )

    def chip_copy(s):
        far = lax.rem(chip + s + 1, chips)
        return remote(
            part.at[2 * s + 1],
            x_in.at[s],
            xs_sem.at[0, s],
            xs_sem.at[1, s],
            {"tp": CORES * far + core},
        )

    def multiply(j):
        @pl.loop(0, tiles)
        def _(n):
            load_w(j, n).wait()
            part[j, :, pl.ds(pl.multiple_of(n * tile, 128), tile)] = jnp.dot(
                x[...], w[j, n], preferred_element_type=f32
            )

    def pass_on(s):
        core_copy(s).wait_recv()
        part[2 * s + 1] = part[2 * s + 1] + core_in[s]
        chip_copy(s).start()

    @pl.loop(0, chips - 1)
    def _(s):
        multiply(2 * s)
        core_copy(s).start()

        @pl.when(s > 0)
        def _():
            pass_on(s - 1)

        multiply(2 * s + 1)

    pass_on(chips - 2)
    own_to(down_kind, start, down_first, range(1, half))

    @pl.when(inner)
    def _():
        relay(down_kind, 1, 0, True, not_from_end)

    multiply(tps - 2)
    core_copy(chips - 1).start()
    multiply(tps - 1)

    own_to(down_kind, wait_send, down_first, range(1, half))

    @pl.when(inner)
    def _():
        relay(down_kind, 1, 0, True, from_end)

    @pl.when(at_end)
    def _():
        local = aid[...] - stored * neighbour
        uses = (local >= 0) & (local < stored)
        below = lax.broadcasted_iota(jnp.int32, (rows, rows), 1) < lax.broadcasted_iota(
            jnp.int32, (rows, rows), 0
        )
        order = jnp.dot(
            jnp.where(below, 1.0, 0.0).astype(bf16),
            jnp.where(uses, 1.0, 0.0).astype(bf16),
            preferred_element_type=f32,
        )
        spot = jnp.where(uses & (order == lane.astype(f32)), 1.0, 0.0)
        place[...] = spot.astype(bf16)
        pick = spot.T.astype(bf16)[:packed]
        row_out[...] = jnp.dot(pick, x[...], preferred_element_type=f32).astype(bf16)
        code_out[...] = jnp.dot(
            pick, local.astype(f32).astype(bf16), preferred_element_type=f32
        ).astype(bf16)
        for c in row_copies():
            c.start()

    @pl.when(at_end)
    def _():
        for a in range(half):
            relay(up_kind, 1, a, True)

    @pl.when(inner)
    def _():
        for a in range(1, half):
            relay(down_kind, 1, a, True, not_from_end)
            relay(down_kind, 1, a, True, from_end, True)

    def shrink(o, h):
        product = lax.dot_general(
            x[...], downs[o, h], (((1,), (1,)), ((), ())), preferred_element_type=f32
        )
        shr[...] += jnp.where(chosen(o, h), product, 0.0)

    shr[...] = jnp.zeros_like(shr)
    load_down.wait()

    def shrink_own(o, side):
        shrink(o, rep)

    @pl.loop(0, reps)
    def _(h):
        shrink(me, h)

    @pl.when(inner)
    def _():
        each_owner(1, shrink_own)

    relay(down_kind, 2, 0, True)
    for a in range(1, half):
        relay(down_kind, 2, a, True)

    @pl.when(at_end)
    def _():
        for c in row_copies():
            c.wait_send()

    own_to(up_kind, start, up_third)
    own_to(up_kind, start, up_second)
    each_owner(2, shrink_own)

    @pl.loop(3, groups)
    def _(k):
        for a in range(half):
            relay(down_kind, k, a, True)
            if a == half - 1:

                @pl.when(k == 3)
                def _():
                    extra_to(down_kind, start, down_extra)

        each_owner(k, shrink_own)

    def shrink_other(k, wanted):
        def visit(owner, side):
            def go():
                receive_other(down_kind, owner, side, k)
                shrink(owner, other_rep)

            pl.when(wanted(owner))(go)

        each_owner(k, visit)

    @pl.when(serves)
    def _():
        for c in row_copies():
            c.wait_recv()
        code = code_in[...].astype(f32).astype(jnp.int32)
        group = lax.div(lax.broadcasted_iota(jnp.int32, (packed, held), 1), rank)
        total = jnp.zeros((packed, held), f32)
        for h in range(reps):
            product = lax.dot_general(
                row_in[...], downs[me, h], (((1,), (1,)), ((), ())), preferred_element_type=f32
            )
            total = total + jnp.where(code == half * h + group, product, 0.0)
        ret_out[...] = total
        ret_copy.start()

    @pl.when(inner)
    def _():
        shrink_other(1, not_from_end)
        for a in range(half):
            relay(up_kind, 1, a, True, not_from_end)
        own_to(up_kind, wait_send, up_second)
        for a in range(half):
            relay(up_kind, 1, a, True, from_end, a > 0)

    @pl.when(at_end)
    def _():
        shrink_other(2, lambda owner: True)
        ret_copy.wait_recv()
        rest = ret_in[...]
        spot = place[...][:, :packed]
        for _ in range(3):
            term = rest.astype(bf16)
            rest = rest - term.astype(f32)
            shr[...] += jnp.dot(spot, term, preferred_element_type=f32)

    for a in range(half):
        relay(up_kind, 2, a, True)
    extra_to(up_kind, start, up_extra)

    @pl.when(inner)
    def _():
        shrink_other(2, lambda owner: True)
        shrink_other(1, from_end)

    @pl.loop(3, groups)
    def _(k):
        shrink_other(k, lambda owner: True)

    block = rows // half
    lane_group = lane_adapter[:block]

    def spread(value):
        total = value
        for g in range(1, half):
            total = total + pltpu.roll(value, g * rank, 1)
        return total

    whole = spread(shr[...])
    pack = jnp.zeros((block, held), f32)
    for g in range(half):
        pack = jnp.where(lane_group == g, whole[g * block : (g + 1) * block], pack)
    shr_own[...] = pack

    shr_core_copy = remote(
        shr_own, shr_core, shr_sem.at[0, chips - 1], shr_sem.at[1, chips - 1], {"tp": other_core}
    )

    def shr_copy(s):
        far = lax.rem(chip + s + 1, chips)
        return remote(
            shr_pair,
            shr_in.at[s],
            shr_sem.at[0, s],
            shr_sem.at[1, s],
            {"tp": CORES * far + core},
        )

    shr_core_copy.start()
    base = part.at[tps - 1]
    core_copy(chips - 1).wait_recv()
    base[...] += core_in[chips - 1]
    shr_core_copy.wait_recv()
    shr_pair[...] = shr_own[...] + shr_core[...]

    @pl.loop(0, chips - 1)
    def _(s):
        shr_copy(s).start()

    @pl.loop(0, chips - 1)
    def _(s):
        chip_copy(s).wait_recv()
        base[...] += x_in[s]

    @pl.loop(3, groups)
    def _(k):
        for a in range(half):
            relay(up_kind, k, a, True)

    shr_own_sum = shr_pair[...]
    for s in range(chips - 1):
        shr_copy(s).wait_recv()
        shr_own_sum = shr_own_sum + shr_in[s]
    for g in range(half):
        shr[g * block : (g + 1) * block] = spread(jnp.where(lane_group == g, shr_own_sum, 0.0))

    def expand(o):
        masks = [chosen(o, h) for h in range(reps)]
        expand_by(masks, ups[o].reshape(reps * held, width))

    def expand_by(masks, up):
        factor = jnp.concatenate(
            [jnp.where(mask, adapter_scale * shr[...], 0.0) for mask in masks], axis=1
        )
        high = factor.astype(bf16)
        low = (factor - high.astype(f32)).astype(bf16)
        base[...] += jnp.dot(high, up, preferred_element_type=f32) + jnp.dot(
            low, up, preferred_element_type=f32
        )

    expand(me)

    @pl.when(at_end)
    def _():
        number = jnp.zeros((rows, held), jnp.int32)
        for e in range(cap):
            number = jnp.where(lane_adapter == e, fetched_ref[me, e, neighbour], number)
        expand_by([aid[...] == stored * neighbour + number], ups[neighbour, rep])

    @pl.when(inner)
    def _():
        def visit(owner, side):
            receive_other(up_kind, owner, side, 1)
            expand(owner)

        each_owner(1, visit)

    @pl.loop(2, groups)
    def _(k):
        def visit(owner, side):
            receive_other(up_kind, owner, side, k)
            expand(owner)

        each_owner(k, visit)

    out_ref[...] = base[...].astype(out_ref.dtype)

    @pl.loop(0, chips)
    def _(s):
        core_copy(s).wait_send()

    @pl.loop(0, chips - 1)
    def _(s):
        chip_copy(s).wait_send()

    @pl.when(serves)
    def _():
        ret_copy.wait_send()

    own_to(up_kind, wait_send, up_third)

    own_to(down_kind, wait_send, down_first, range(1))
    extra_to(down_kind, wait_send, down_extra)
    own_to(up_kind, wait_send, up_first, source=picked)
    shr_core_copy.wait_send()

    @pl.loop(0, chips - 1)
    def _(s):
        shr_copy(s).wait_send()

    extra_to(up_kind, wait_send, up_extra)

    @pl.loop(1, groups)
    def _(k):
        for kind in (down_kind, up_kind):
            for a in range(half):
                relay(kind, k, a, False)


def body(
    sizes,
    attention_input,
    output_weight,
    adapter_down_weight,
    adapter_up_weight,
    fetched_local_numbers,
    request_adapter_entry,
):
    reps, groups, tps = sizes
    chips = tps // CORES
    rows, features = attention_input.shape
    stored, _, rank = adapter_down_weight.shape
    width = adapter_up_weight.shape[2]
    half = stored // reps
    held = half * rank
    tile = min(512, width)
    tiles = width // tile
    down = adapter_down_weight.transpose(0, 2, 1).reshape(reps, held, features)
    up = adapter_up_weight.reshape(reps, held, width)
    cap = fetched_local_numbers.shape[2]
    packed = rows * cap // groups
    any_space = pl.BlockSpec(memory_space=pl.ANY)
    vmem = pl.BlockSpec(memory_space=pltpu.VMEM)
    dma = pltpu.SemaphoreType.DMA
    f32, bf16 = jnp.float32, jnp.bfloat16
    return pl.pallas_call(
        functools.partial(kernel, (reps, groups, tps, rank)),
        out_shape=pltpu.VMEM((rows, width), bf16),
        in_specs=[vmem, pl.BlockSpec(memory_space=pltpu.SMEM)] + [any_space] * 4,
        out_specs=vmem,
        scratch_shapes=[
            pltpu.VMEM((rows, features), bf16),
            pltpu.VMEM((tps, tiles, features, tile), bf16),
            pltpu.VMEM((groups, reps, held, features), bf16),
            pltpu.VMEM((groups, reps, held, width), bf16),
            pltpu.VMEM((tps, rows, width), f32),
            pltpu.VMEM((chips, rows, width), f32),
            pltpu.VMEM((chips - 1, rows, width), f32),
            pltpu.VMEM((rows, held), f32),
            pltpu.VMEM((rows // half, held), f32),
            pltpu.VMEM((rows // half, held), f32),
            pltpu.VMEM((rows // half, held), f32),
            pltpu.VMEM((chips - 1, rows // half, held), f32),
            pltpu.VMEM((held, width), bf16),
            pltpu.VMEM((rows, held), jnp.int32),
            pltpu.VMEM((rows, held), bf16),
            pltpu.VMEM((packed, features), bf16),
            pltpu.VMEM((packed, features), bf16),
            pltpu.VMEM((packed, held), bf16),
            pltpu.VMEM((packed, held), bf16),
            pltpu.VMEM((packed, held), f32),
            pltpu.VMEM((packed, held), f32),
            dma((3,)),
            dma((tps, tiles)),
            dma((2, chips)),
            dma((2, chips - 1)),
            dma((2, chips)),
            dma((3, groups, half)),
            dma((2, groups, half)),
            dma((4, half)),
            dma((3, groups, half)),
            dma((2, groups, half)),
            dma((4, half)),
            dma((6,)),
        ],
        compiler_params=pltpu.CompilerParams(
            collective_id=0, has_side_effects=True, vmem_limit_bytes=56 * 1024 * 1024
        ),
    )(
        request_adapter_entry,
        fetched_local_numbers.transpose(0, 2, 1),
        attention_input,
        output_weight,
        down,
        up,
    )


def solution(mesh):
    in_specs = (
        P(("rep", "dp"), "tp"),
        P("tp", None),
        P("dp", "tp", None),
        P("dp", None, "tp"),
        P("rep", None, None),
        P(("rep", "dp")),
    )
    out_specs = P(("rep", "dp"), "tp")
    sizes = (mesh.shape["rep"], mesh.shape["dp"], mesh.shape["tp"])
    return jax.shard_map(
        functools.partial(body, sizes),
        mesh=mesh,
        in_specs=in_specs,
        out_specs=out_specs,
        check_vma=False,
    )
```
